256 devices in a mesh: context: 32 (over z, x), tensor: 8 (over y, core).
Axes of the slice: x: 4, y: 4, z: 8, core: 2. Of those that a mesh axis runs over, the one named last changes fastest.
Arguments:
- query_proj: bfloat16 [4096, 16384], P('tensor', 'context'), may hold values from -6 to 6
- key_proj: bfloat16 [4096, 16384], P('tensor', 'context'), may hold values from -6 to 6
- value_proj: bfloat16 [4096, 16384], P('tensor', 'context'), may hold values from -6 to 6
- short_weight: float32 [3, 3, 4096], P(None, None, 'tensor'), may hold values from -3 to 3
- skip_bias: float32 [4096], P('tensor'), may hold values from -4 to 4
- filter_taps: float32 [8, 16384], P('tensor', 'context'), may hold values from -1.4 to 1.4
Outputs:
- mixed: bfloat16 [4096, 16384], P('tensor', 'context')
The draws below stay inside these ranges and needn't reach their ends.
All inputs are finite; a program needn't handle non-finite values.
Results may differ from the reference program's by a relative error of at most 0.001.
Values may be sent and summed in bfloat16 or wider, within the bound.
No kernel may reach another device: no remote copies, remote signals or barrier semaphores. Data moves between devices by JAX's collectives and lax.ppermute only.
A program may use at most 128 MiB of HBM per device.

```python
import math
import jax
import jax.numpy as jnp
from jax import lax

FILT = 8
SHORT = 3
SEQ = 16384
CH = 4096


def draw_filter_taps(key, part):
    key = jax.random.fold_in(key, 11)
    first_key, second_key = jax.random.split(key)
    decay_spans = jnp.exp(jax.random.uniform(first_key, (FILT, 1), jnp.float32, math.log(40.0), math.log(4.0 * SEQ)))
    rough_part = jnp.clip(jax.random.normal(second_key, (FILT, SEQ), jnp.float32), -6.0, 6.0)
    steps = jnp.arange(SEQ, dtype=jnp.float32)[None, :]
    return rough_part * jnp.exp(-steps / decay_spans) * jnp.sqrt(1.0 - jnp.exp(-2.0 / decay_spans))


def levels(rng, dims, cuts, smallest, top_value):
    level = 1.0
    for position, blocks in cuts:
        heights = jax.random.uniform(jax.random.fold_in(jax.random.fold_in(rng, 6), position), (blocks,), jnp.float32, smallest / len(cuts), top_value / len(cuts))
        level = level * jnp.repeat(jnp.exp(heights), dims[position] // blocks).reshape((-1,) + (1,) * (len(dims) - 1 - position))
    return level


def bell_draw(own_key, dims, spread, most, cuts=(), kind=jnp.bfloat16):
    result = spread * jax.random.normal(own_key, dims, jnp.float32)
    if cuts:
        result = result * levels(own_key, dims, cuts, -0.22, 0.18)
    return jnp.clip(result, -most, most).astype(kind)


def setup_inputs(seed: int = 0) -> dict:
    seeds = jax.random.split(jax.random.key(seed), 7)
    return {
        "query_proj": bell_draw(seeds[0], (CH, SEQ), 1.0, 6.0, ((0, 8), (1, 32))),
        "key_proj": bell_draw(seeds[1], (CH, SEQ), 1.0, 6.0, ((0, 8), (1, 32))),
        "value_proj": bell_draw(seeds[2], (CH, SEQ), 1.0, 6.0, ((0, 8), (1, 32))),
        "short_weight": bell_draw(seeds[3], (3, SHORT, CH), 0.6, 3.0, ((2, 8),), jnp.float32),
        "skip_bias": bell_draw(seeds[4], (CH,), 1.0, 4.0, ((0, 8),), jnp.float32),
        "filter_taps": draw_filter_taps(jax.random.fold_in(seeds[6], 71), 0),
    }


def short_mix(stream, weights):
    taps_count = weights.shape[0]
    length = stream.shape[1]
    padded = jnp.pad(stream.astype(jnp.float32), ((0, 0), (taps_count - 1, 0)))
    summed = weights[0][:, None] * padded[:, taps_count - 1:]
    for lag_step in range(1, taps_count):
        start_col = taps_count - 1 - lag_step
        summed = summed + weights[lag_step][:, None] * padded[:, start_col:start_col + length]
    return summed


def reference(query_proj, key_proj, value_proj, short_weight, skip_bias, filter_taps):
    query_short = short_mix(query_proj, short_weight[0])
    key_short = short_mix(key_proj, short_weight[1])
    value_short = short_mix(value_proj, short_weight[2])
    product_in = key_short * value_short
    filter_spec = jnp.fft.rfft(filter_taps, n=2 * SEQ, axis=1)
    groups = product_in.reshape(CH // FILT, FILT, SEQ)

    def convolve(channel_group):
        spectrum = jnp.fft.rfft(channel_group, n=2 * SEQ, axis=1) * filter_spec
        return jnp.fft.irfft(spectrum, n=2 * SEQ, axis=1)[:, :SEQ].astype(product_in.dtype)

    long_conv = lax.map(convolve, groups).reshape(CH, SEQ)
    mixed = query_short * (long_conv + skip_bias[:, None] * product_in)
    return mixed.astype(jnp.bfloat16)
```

```python
import jax
import jax.numpy as jnp
from jax import lax
from jax.experimental import pallas as pl
from jax.experimental.pallas import tpu as pltpu
from jax.sharding import PartitionSpec as P

FILT = 8
TILE = 128
ROWS = 16
CHUNK = 72
GAIN = 16.0
SLOPE = 61.0
LIFT = 125.0
TINY = 1e-30
MIB = 1024 * 1024


def scale_of(peak):
    return jnp.maximum(peak, TINY).astype(jnp.bfloat16).astype(jnp.float32)


def encode(values, scale):
    level = jnp.log2(1.0 + jnp.abs(values) * (GAIN / scale))
    size = jnp.exp2(level * SLOPE - LIFT)
    return jnp.where(values < 0.0, -size, size)


def decode(codes, scale):
    level = (jnp.log2(jnp.abs(codes)) + LIFT) * (1.0 / SLOPE)
    size = (jnp.exp2(level) - 1.0) * (scale * (1.0 / GAIN))
    return jnp.where(codes < 0.0, -size, size)


def split(values):
    high = values.astype(jnp.bfloat16)
    low = (values - high.astype(jnp.float32)).astype(jnp.bfloat16)
    return high, low


def short_mix(stream, before, weights):
    length = stream.shape[1]
    lane = lax.broadcasted_iota(jnp.int32, stream.shape, 1)
    one = pltpu.roll(stream, 1, 1)
    one = jnp.where(lane == 0, before[:, 1:2], one)
    two = pltpu.roll(stream, 2, 1)
    two = jnp.where(lane == 0, before[:, 0:1], jnp.where(lane == 1, before[:, 1:2], two))
    return weights[0] * stream + weights[1] * one + weights[2] * two


def to_lanes(column):
    shape = (TILE, TILE)
    lane = lax.broadcasted_iota(jnp.int32, shape, 1)
    group = lax.broadcasted_iota(jnp.int32, shape, 0) // FILT
    spread = jnp.where(lane == group, column, 0.0)
    return spread.reshape(ROWS, FILT, TILE).sum(axis=0)


def front_kernel(key_ref, value_ref, side_ref, taps_ref, prod_ref, out_ref, coded):
    side = jnp.transpose(side_ref[...])
    key = key_ref[...].astype(jnp.float32)
    value = value_ref[...].astype(jnp.float32)
    key_short = short_mix(key, side[:, 10:12], [side[:, n : n + 1] for n in range(3, 6)])
    value_short = short_mix(value, side[:, 12:14], [side[:, n : n + 1] for n in range(6, 9)])
    product = key_short * value_short
    prod_ref[...] = product
    scale = scale_of(jnp.max(jnp.abs(product), axis=1, keepdims=True))
    coded_rows = encode(product, scale)
    for block in range(4):
        coded[block] = coded_rows[:, block * TILE : (block + 1) * TILE]
    scales = to_lanes(scale)
    row = lax.broadcasted_iota(jnp.int32, (8, TILE), 0)
    for filt in range(FILT):
        for block in range(4):
            part = coded[block, pl.ds(filt, ROWS, stride=FILT), :]
            out_ref[filt, pl.ds(block * ROWS, ROWS), :] = part.astype(jnp.bfloat16)
        taps = taps_ref[filt]
        tap_scale = scale_of(jnp.max(jnp.abs(taps)))
        tail = encode(taps, tap_scale)
        tail = jnp.where(row == 4, scales[filt : filt + 1, :], tail)
        tail = jnp.where(row == 5, tap_scale, tail)
        out_ref[filt, pl.ds(64, 8), :] = tail.astype(jnp.bfloat16)


def conv_kernel(in_ref, out_ref, high, low, taps, toep_high, toep_low, total):
    count = in_ref.shape[0]
    lane = lax.broadcasted_iota(jnp.int32, (ROWS, TILE), 1)
    row = lax.broadcasted_iota(jnp.int32, (ROWS, TILE), 0)

    def unpack(src, carry):
        tail = in_ref[src, pl.ds(64, 8), :].astype(jnp.float32)
        scale = jnp.sum(jnp.where(lane == row, tail[4:5, :], 0.0), axis=1, keepdims=True)
        taps[pl.ds(src * 4, 4), :] = decode(tail[0:4, :], tail[5:6, :])
        for block in range(4):
            part = in_ref[src, pl.ds(block * ROWS, ROWS), :].astype(jnp.float32)
            upper, lower = split(decode(part, scale))
            at = pl.ds(pl.multiple_of(src * 32 + (block // 2) * ROWS, ROWS), ROWS)
            cols = pl.ds((block % 2) * TILE, TILE)
            high[at, cols] = upper
            low[at, cols] = lower
        return carry

    lax.fori_loop(0, count, unpack, 0)
    wide_lane = lax.broadcasted_iota(jnp.int32, (TILE, TILE), 1)
    wide_row = lax.broadcasted_iota(jnp.int32, (TILE, TILE), 0)
    causal = wide_lane >= wide_row
    zero = jnp.zeros((TILE, TILE), jnp.bfloat16)
    toep_high[0] = zero
    toep_low[0] = zero

    def build(tile, before):
        line = jnp.broadcast_to(taps[pl.ds(tile, 1), :], (TILE, TILE))
        rolled = pltpu.roll(line, 0, 1, stride=1, stride_axis=0)
        upper, lower = split(jnp.where(causal, rolled, before))
        toep_high[tile + 1] = upper
        toep_low[tile + 1] = lower
        return rolled

    lax.fori_loop(0, count * 4, build, jnp.zeros((TILE, TILE), jnp.float32))
    blocks = count * 2
    size = blocks * ROWS

    def weight(ref, lag):
        top = jnp.concatenate([ref[2 * lag + 1], ref[2 * lag + 2]], axis=1)
        bottom = jnp.concatenate([ref[2 * lag], ref[2 * lag + 1]], axis=1)
        return jnp.concatenate([top, bottom], axis=0)

    for lag in range(blocks):
        rows = size - lag * ROWS
        upper = weight(toep_high, lag)
        lower = weight(toep_low, lag)
        left = jnp.concatenate([high[:rows, :], low[:rows, :], high[:rows, :]], axis=1)
        right = jnp.concatenate([upper, upper, lower], axis=0)
        part = jnp.dot(left, right, preferred_element_type=jnp.float32)
        if lag == 0:
            total[...] = part
        else:
            total[lag * ROWS :, :] += part

    pick = lax.broadcasted_iota(jnp.int32, (8, TILE), 0) == 0

    def pack(dst, carry):
        parts = []
        for block in range(4):
            at = pl.ds(pl.multiple_of(dst * 32 + (block // 2) * ROWS, ROWS), ROWS)
            parts.append(total[at, pl.ds((block % 2) * TILE, TILE)])
        peak = jnp.max(jnp.abs(parts[0]), axis=1, keepdims=True)
        for part in parts[1:]:
            peak = jnp.maximum(peak, jnp.max(jnp.abs(part), axis=1, keepdims=True))
        scale = scale_of(peak)
        for block in range(4):
            codes = encode(parts[block], scale).astype(jnp.bfloat16)
            out_ref[dst, pl.ds(block * ROWS, ROWS), :] = codes
        spread = jnp.sum(jnp.where(lane == row, scale, 0.0), axis=0, keepdims=True)
        out_ref[dst, pl.ds(64, 8), :] = jnp.where(pick, spread, 0.0).astype(jnp.bfloat16)
        return carry

    lax.fori_loop(0, count, pack, 0)


def back_kernel(in_ref, query_ref, side_ref, prod_ref, out_ref, plain):
    lane = lax.broadcasted_iota(jnp.int32, (ROWS, TILE), 1)
    row = lax.broadcasted_iota(jnp.int32, (ROWS, TILE), 0)
    for filt in range(FILT):
        tail = in_ref[filt, pl.ds(64, 8), :].astype(jnp.float32)
        scale = jnp.sum(jnp.where(lane == row, tail[0:1, :], 0.0), axis=1, keepdims=True)
        for block in range(4):
            part = in_ref[filt, pl.ds(block * ROWS, ROWS), :].astype(jnp.float32)
            plain[block, pl.ds(filt, ROWS, stride=FILT), :] = decode(part, scale)
    side = jnp.transpose(side_ref[...])
    query = query_ref[...].astype(jnp.float32)
    query_short = short_mix(query, side[:, 14:16], [side[:, n : n + 1] for n in range(3)])
    long = jnp.concatenate([plain[block] for block in range(4)], axis=1)
    mixed = query_short * (long + side[:, 9:10] * prod_ref[...])
    out_ref[...] = mixed.astype(jnp.bfloat16)


def front(key_proj, value_proj, side, taps):
    rows, length = key_proj.shape
    steps = rows // TILE
    stream = pl.BlockSpec((TILE, length), lambda n: (n, 0))
    return pl.pallas_call(
        front_kernel,
        grid=(steps,),
        in_specs=[
            stream,
            stream,
            pl.BlockSpec((16, TILE), lambda n: (0, n)),
            pl.BlockSpec((FILT, 8, TILE), lambda n: (0, 0, 0)),
        ],
        out_specs=[stream, pl.BlockSpec((FILT, CHUNK, TILE), lambda n: (n, 0, 0))],
        out_shape=[
            jax.ShapeDtypeStruct((rows, length), jnp.float32),
            jax.ShapeDtypeStruct((steps * FILT, CHUNK, TILE), jnp.bfloat16),
        ],
        scratch_shapes=[pltpu.VMEM((4, TILE, TILE), jnp.float32)],
        compiler_params=pltpu.CompilerParams(vmem_limit_bytes=16 * MIB),
        name="front",
    )(key_proj, value_proj, side, taps)


def conv(chunks):
    count = chunks.shape[0]
    size = count * 2 * ROWS
    whole = pl.BlockSpec(memory_space=pltpu.VMEM)
    return pl.pallas_call(
        conv_kernel,
        in_specs=[whole],
        out_specs=whole,
        out_shape=jax.ShapeDtypeStruct(chunks.shape, jnp.bfloat16),
        scratch_shapes=[
            pltpu.VMEM((size, 2 * TILE), jnp.bfloat16),
            pltpu.VMEM((size, 2 * TILE), jnp.bfloat16),
            pltpu.VMEM((count * 4, TILE), jnp.float32),
            pltpu.VMEM((count * 4 + 1, TILE, TILE), jnp.bfloat16),
            pltpu.VMEM((count * 4 + 1, TILE, TILE), jnp.bfloat16),
            pltpu.VMEM((size, 2 * TILE), jnp.float32),
        ],
        compiler_params=pltpu.CompilerParams(vmem_limit_bytes=40 * MIB),
        name="conv",
    )(chunks)


def back(chunks, query_proj, side, product):
    rows, length = query_proj.shape
    steps = rows // TILE
    stream = pl.BlockSpec((TILE, length), lambda n: (n, 0))
    return pl.pallas_call(
        back_kernel,
        grid=(steps,),
        in_specs=[
            pl.BlockSpec((FILT, CHUNK, TILE), lambda n: (n, 0, 0)),
            stream,
            pl.BlockSpec((16, TILE), lambda n: (0, n)),
            stream,
        ],
        out_specs=stream,
        out_shape=jax.ShapeDtypeStruct((rows, length), jnp.bfloat16),
        scratch_shapes=[pltpu.VMEM((4, TILE, TILE), jnp.float32)],
        compiler_params=pltpu.CompilerParams(vmem_limit_bytes=16 * MIB),
        name="back",
    )(chunks, query_proj, side, product)


def local(query_proj, key_proj, value_proj, short_weight, skip_bias, filter_taps):
    count = lax.axis_size("context")
    rows = query_proj.shape[0]
    rim = jnp.concatenate(
        [stream[:, -2:].T for stream in (key_proj, value_proj, query_proj)], axis=0
    )
    pairs = [(n, n + 1) for n in range(count - 1)]
    rim = lax.ppermute(rim, "context", pairs).astype(jnp.float32)
    side = jnp.concatenate([short_weight.reshape(9, rows), skip_bias[None, :], rim], axis=0)
    taps = jnp.pad(filter_taps.reshape(1, 4, TILE), ((0, 0), (0, 4), (0, 0)))
    taps = jnp.broadcast_to(taps, (FILT, 8, TILE))
    taps = lax.all_to_all(taps, "tensor", 0, 0, tiled=True)
    product, chunks = front(key_proj, value_proj, side, taps)
    chunks = lax.all_to_all(chunks, "context", 0, 0, tiled=True)
    chunks = conv(chunks)
    chunks = lax.all_to_all(chunks, "context", 0, 0, tiled=True)
    return back(chunks, query_proj, side, product)


def solution(mesh):
    in_specs = (
        P("tensor", "context"),
        P("tensor", "context"),
        P("tensor", "context"),
        P(None, None, "tensor"),
        P("tensor"),
        P("tensor", "context"),
    )
    out_specs = P("tensor", "context")
    return jax.shard_map(local, mesh=mesh, in_specs=in_specs, out_specs=out_specs, check_vma=False)
```

```python
import jax
import jax.numpy as jnp
from jax import lax
from jax.experimental import pallas as pl
from jax.experimental.pallas import tpu as pltpu
from jax.sharding import PartitionSpec as P

FILT = 8
TILE = 128
ROWS = 16
CHUNK = 72
GAIN = 16.0
SLOPE = 61.0
LIFT = 125.0
TINY = 1e-30
MIB = 1024 * 1024


def scale_of(peak):
    return jnp.maximum(peak, TINY).astype(jnp.bfloat16).astype(jnp.float32)


def encode(values, scale):
    level = jnp.log2(1.0 + jnp.abs(values) * (GAIN / scale))
    size = jnp.exp2(level * SLOPE - LIFT)
    return jnp.where(values < 0.0, -size, size)


def decode(codes, scale):
    level = (jnp.log2(jnp.abs(codes)) + LIFT) * (1.0 / SLOPE)
    size = (jnp.exp2(level) - 1.0) * (scale * (1.0 / GAIN))
    return jnp.where(codes < 0.0, -size, size)


def split(values):
    high = values.astype(jnp.bfloat16)
    low = (values - high.astype(jnp.float32)).astype(jnp.bfloat16)
    return high, low


def short_mix(stream, before, weights):
    length = stream.shape[1]
    lane = lax.broadcasted_iota(jnp.int32, stream.shape, 1)
    one = pltpu.roll(stream, 1, 1)
    one = jnp.where(lane == 0, before[:, 1:2], one)
    two = pltpu.roll(stream, 2, 1)
    two = jnp.where(lane == 0, before[:, 0:1], jnp.where(lane == 1, before[:, 1:2], two))
    return weights[0] * stream + weights[1] * one + weights[2] * two


def to_lanes(column):
    shape = (TILE, TILE)
    lane = lax.broadcasted_iota(jnp.int32, shape, 1)
    group = lax.broadcasted_iota(jnp.int32, shape, 0) // FILT
    spread = jnp.where(lane == group, column, 0.0)
    return spread.reshape(ROWS, FILT, TILE).sum(axis=0)


def edge_kernel(key_ref, value_ref, query_ref, out_ref, ends, arrived):
    length = key_ref.shape[1]
    copies = []
    for place, ref in enumerate((key_ref, value_ref, query_ref)):
        source = ref.at[:, pl.ds(length - TILE, TILE)]
        copies.append(pltpu.make_async_copy(source, ends.at[place], arrived.at[place]))
        copies[-1].start()
    row = lax.broadcasted_iota(jnp.int32, (8, TILE), 0)
    lane = lax.broadcasted_iota(jnp.int32, (8, TILE), 1)
    total = None
    for place, copy in enumerate(copies):
        copy.wait()
        pick = (row // 2 == place) & (lane == TILE - 2 + row % 2)
        part = lax.dot_general(
            pick.astype(jnp.bfloat16),
            ends[place],
            (((1,), (1,)), ((), ())),
            preferred_element_type=jnp.float32,
        )
        total = part if total is None else total + part
    out_ref[...] = total


def side_columns(weight_ref, skip_ref, rim_ref, cols):
    rows = [weight_ref[:, cols], skip_ref[:, cols], rim_ref[:6, cols]]
    return jnp.transpose(jnp.concatenate(rows, axis=0))


def product_of(key_ref, value_ref, side, rows):
    key = key_ref[rows, :].astype(jnp.float32)
    value = value_ref[rows, :].astype(jnp.float32)
    key_short = short_mix(key, side[:, 10:12], [side[:, n : n + 1] for n in range(3, 6)])
    value_short = short_mix(value, side[:, 12:14], [side[:, n : n + 1] for n in range(6, 9)])
    return key_short * value_short


def front_kernel(key_ref, value_ref, weight_ref, skip_ref, rim_ref, coded_ref, scale_ref):
    for step in range(key_ref.shape[0] // TILE):
        rows = slice(step * TILE, (step + 1) * TILE)
        side = side_columns(weight_ref, skip_ref, rim_ref, rows)
        product = product_of(key_ref, value_ref, side, rows)
        scale = scale_of(jnp.max(jnp.abs(product), axis=1, keepdims=True))
        coded_rows = encode(product, scale)
        for block in range(4):
            coded_ref[block, rows, :] = coded_rows[:, block * TILE : (block + 1) * TILE]
        scale_ref[step * FILT : (step + 1) * FILT, :] = to_lanes(scale)


def deal_kernel(coded_ref, scale_ref, taps_ref, out_ref):
    row = lax.broadcasted_iota(jnp.int32, (8, TILE), 0)
    tails = []
    for filt in range(FILT):
        taps = taps_ref[filt]
        tap_scale = scale_of(jnp.max(jnp.abs(taps)))
        tail = jnp.where(row == 5, tap_scale, 0.0)
        codes = encode(taps, tap_scale)
        for block in range(4):
            part = codes[:, block * TILE : (block + 1) * TILE]
            tail = jnp.where(row == block, part, tail)
        tails.append(tail)
    for dest in range(out_ref.shape[0]):
        step, filt = dest // FILT, dest % FILT
        for block in range(4):
            rows = pl.ds(step * TILE + filt, ROWS, stride=FILT)
            part = coded_ref[block, rows, :]
            out_ref[dest, block * ROWS : (block + 1) * ROWS, :] = part.astype(jnp.bfloat16)
        tail = jnp.where(row == 4, scale_ref[dest : dest + 1, :], tails[filt])
        out_ref[dest, 64:72, :] = tail.astype(jnp.bfloat16)


def gate_rows(streams, side, rows, local, query_out, base_out):
    query_ref, key_ref, value_ref = streams
    side = side[local, :]
    query = query_ref[rows, :].astype(jnp.float32)
    query_short = short_mix(query, side[:, 14:16], [side[:, n : n + 1] for n in range(3)])
    query_out[rows, :] = query_short
    product = product_of(key_ref, value_ref, side, rows)
    base_out[rows, :] = query_short * (side[:, 9:10] * product)


FINE = 512.0
GATE_FROM = 4


def unit_of(peak):
    power = jnp.exp2(7.0 - jnp.ceil(jnp.log2(jnp.maximum(peak, TINY))))
    return power.astype(jnp.bfloat16).astype(jnp.float32)


def four_parts(values):
    coarse = values.astype(jnp.bfloat16)
    wide = coarse.astype(jnp.float32)
    narrow = wide.astype(jnp.float8_e4m3fn)
    fine = ((values - wide) * FINE).astype(jnp.float8_e4m3fn)
    return coarse, narrow, fine


def conv_kernel(
    in_ref,
    query_ref,
    key_ref,
    value_ref,
    weight_ref,
    skip_ref,
    rim_ref,
    out_ref,
    query_out,
    base_out,
    main,
    cross,
    taps,
    toep,
    toep_narrow,
    toep_fine,
    total,
    back_unit,
):
    streams = (query_ref, key_ref, value_ref)
    count = in_ref.shape[0]
    blocks = count * 2
    size = blocks * ROWS
    lane = lax.broadcasted_iota(jnp.int32, (ROWS, TILE), 1)
    row = lax.broadcasted_iota(jnp.int32, (ROWS, TILE), 0)
    diagonal = lane == row
    pick = lax.broadcasted_iota(jnp.int32, (8, TILE), 0) == 0
    wide_lane = lax.broadcasted_iota(jnp.int32, (TILE, TILE), 1)
    causal = wide_lane >= lax.broadcasted_iota(jnp.int32, (TILE, TILE), 0)

    def tail_of(src):
        return in_ref[src, pl.ds(64, 8), :].astype(jnp.float32)

    peaks = tail_of(0)
    for src in range(1, count):
        peaks = jnp.maximum(peaks, tail_of(src))
    unit = unit_of(jnp.sum(jnp.where(diagonal, peaks[4:5, :], 0.0), axis=1, keepdims=True))
    tap_unit = unit_of(peaks[5:6, 0:1])
    back_unit[...] = jnp.broadcast_to(1.0 / (unit * tap_unit), (ROWS, TILE))

    def unpack(src, carry):
        tail = tail_of(src)
        scale = jnp.sum(jnp.where(diagonal, tail[4:5, :], 0.0), axis=1, keepdims=True) * unit
        taps[pl.ds(src * 4, 4), :] = decode(tail[0:4, :], tail[5:6, :] * tap_unit)
        at = pl.ds(pl.multiple_of(src * 32, 32), 32)
        for half in range(2):
            pair = []
            for block in (half, half + 2):
                part = in_ref[src, pl.ds(block * ROWS, ROWS), :].astype(jnp.float32)
                pair.append(decode(part, scale))
            coarse, narrow, fine = four_parts(jnp.concatenate(pair, axis=0))
            main[at, pl.ds(half * TILE, TILE)] = coarse
            cross[at, pl.ds(half * TILE, TILE)] = fine
            cross[at, pl.ds((half + 2) * TILE, TILE)] = narrow
        return carry

    def build(tile, before):
        line = jnp.broadcast_to(taps[tile : tile + 1, :], (TILE, TILE))
        rolled = pltpu.roll(line, 0, 1, stride=1, stride_axis=0)
        coarse, narrow, fine = four_parts(jnp.where(causal, rolled, before))
        toep[tile + 1] = coarse
        toep_narrow[tile + 1] = narrow
        toep_fine[tile + 1] = fine
        return rolled

    def weight(ref, lag):
        top = jnp.concatenate([ref[2 * lag + 1], ref[2 * lag + 2]], axis=1)
        bottom = jnp.concatenate([ref[2 * lag], ref[2 * lag + 1]], axis=1)
        return jnp.concatenate([top, bottom], axis=0)

    def pack(dst):
        parts = []
        for block in range(4):
            at = pl.ds(dst * 32 + (block // 2) * ROWS, ROWS)
            parts.append(total[at, pl.ds((block % 2) * TILE, TILE)])
        peak = jnp.maximum(
            jnp.maximum(jnp.abs(parts[0]), jnp.abs(parts[1])),
            jnp.maximum(jnp.abs(parts[2]), jnp.abs(parts[3])),
        )
        scale = scale_of(jnp.max(peak, axis=1, keepdims=True))
        for block in range(4):
            codes = encode(parts[block], scale).astype(jnp.bfloat16)
            out_ref[dst, pl.ds(block * ROWS, ROWS), :] = codes
        sent = jnp.where(diagonal, scale * back_unit[...], 0.0)
        spread = jnp.sum(sent, axis=0, keepdims=True)
        out_ref[dst, pl.ds(64, 8), :] = jnp.where(pick, spread, 0.0).astype(jnp.bfloat16)

    lax.fori_loop(0, count, unpack, 0, unroll=8)
    toep[0] = jnp.zeros((TILE, TILE), toep.dtype)
    toep_narrow[0] = jnp.zeros((TILE, TILE), toep_narrow.dtype)
    toep_fine[0] = jnp.zeros((TILE, TILE), toep_fine.dtype)
    rolled = build(1, build(0, jnp.zeros((TILE, TILE), jnp.float32)))
    for lag in range(blocks):
        if lag + 1 < blocks:
            rolled = build(2 * lag + 3, build(2 * lag + 2, rolled))
        rows = size - lag * ROWS
        part = jnp.dot(main[:rows, :], weight(toep, lag), preferred_element_type=jnp.float32)
        narrow = jnp.concatenate([weight(toep_narrow, lag), weight(toep_fine, lag)], axis=0)
        rest = jnp.dot(cross[:rows, :], narrow, preferred_element_type=jnp.float32)
        part = part + rest * (1.0 / FINE)
        if lag == 0:
            total[...] = part
        else:
            total[lag * ROWS :, :] += part
        if lag % 2 == 1:
            pack(lag // 2)
        if GATE_FROM <= lag < GATE_FROM + 3 * 16 and (lag - GATE_FROM) % 3 == 0:
            piece = (lag - GATE_FROM) // 3
            if piece % 4 == 0:
                cols = slice(piece * 32, piece * 32 + TILE)
                side = side_columns(weight_ref, skip_ref, rim_ref, cols)
            rows = slice(piece * 32, (piece + 1) * 32)
            local_rows = slice(piece % 4 * 32, piece % 4 * 32 + 32)
            gate_rows(streams, side, rows, local_rows, query_out, base_out)


def conv(chunks, streams, weight, skip, rim):
    count = chunks.shape[0]
    plane = jax.ShapeDtypeStruct(streams[0].shape, jnp.float32)
    size = count * 2 * ROWS
    tiles = (count * 4 + 1, TILE, TILE)
    whole = pl.BlockSpec(memory_space=pltpu.VMEM)
    return pl.pallas_call(
        conv_kernel,
        in_specs=[whole] * 7,
        out_specs=[whole] * 3,
        out_shape=[jax.ShapeDtypeStruct(chunks.shape, jnp.bfloat16), plane, plane],
        scratch_shapes=[
            pltpu.VMEM((size, 2 * TILE), jnp.bfloat16),
            pltpu.VMEM((size, 4 * TILE), jnp.float8_e4m3fn),
            pltpu.VMEM((count * 4, TILE), jnp.float32),
            pltpu.VMEM(tiles, jnp.bfloat16),
            pltpu.VMEM(tiles, jnp.float8_e4m3fn),
            pltpu.VMEM(tiles, jnp.float8_e4m3fn),
            pltpu.VMEM((size, 2 * TILE), jnp.float32),
            pltpu.VMEM((ROWS, TILE), jnp.float32),
        ],
        compiler_params=pltpu.CompilerParams(vmem_limit_bytes=24 * MIB),
        name="conv",
    )(chunks, *streams, weight, skip, rim)


def back_kernel(in_ref, query_ref, base_ref, out_ref, plain):
    lane = lax.broadcasted_iota(jnp.int32, (ROWS, TILE), 1)
    row = lax.broadcasted_iota(jnp.int32, (ROWS, TILE), 0)
    step = pl.program_id(0)
    for filt in range(FILT):
        src = step * FILT + filt
        tail = in_ref[src, pl.ds(64, 8), :].astype(jnp.float32)
        scale = jnp.sum(jnp.where(lane == row, tail[0:1, :], 0.0), axis=1, keepdims=True)
        for block in range(4):
            part = in_ref[src, pl.ds(block * ROWS, ROWS), :].astype(jnp.float32)
            plain[block, pl.ds(filt, ROWS, stride=FILT), :] = decode(part, scale)
    rows = pl.ds(pl.multiple_of(step * TILE, TILE), TILE)
    long = jnp.concatenate([plain[block] for block in range(4)], axis=1)
    out_ref[...] = (query_ref[rows, :] * long + base_ref[rows, :]).astype(jnp.bfloat16)


WHOLE = pl.BlockSpec(memory_space=pltpu.VMEM)


def whole_call(kernel, name, outs, *operands):
    return pl.pallas_call(
        kernel,
        in_specs=[WHOLE] * len(operands),
        out_specs=[WHOLE] * len(outs),
        out_shape=[jax.ShapeDtypeStruct(shape, dtype) for shape, dtype in outs],
        compiler_params=pltpu.CompilerParams(vmem_limit_bytes=16 * MIB),
        name=name,
    )(*operands)


def edge(key_proj, value_proj, query_proj):
    rows = key_proj.shape[0]
    return pl.pallas_call(
        edge_kernel,
        in_specs=[pl.BlockSpec(memory_space=pl.ANY)] * 3,
        out_specs=WHOLE,
        out_shape=jax.ShapeDtypeStruct((8, rows), jnp.float32),
        scratch_shapes=[
            pltpu.VMEM((3, rows, TILE), key_proj.dtype),
            pltpu.SemaphoreType.DMA((3,)),
        ],
        name="edge",
    )(key_proj, value_proj, query_proj)


def back(chunks, query_short, base):
    rows, length = base.shape
    return pl.pallas_call(
        back_kernel,
        grid=(rows // TILE,),
        in_specs=[WHOLE] * 3,
        out_specs=pl.BlockSpec((TILE, length), lambda n: (n, 0)),
        out_shape=jax.ShapeDtypeStruct((rows, length), jnp.bfloat16),
        scratch_shapes=[pltpu.VMEM((4, TILE, TILE), jnp.float32)],
        compiler_params=pltpu.CompilerParams(vmem_limit_bytes=16 * MIB),
        name="back",
    )(chunks, query_short, base)


def local(query_proj, key_proj, value_proj, short_weight, skip_bias, filter_taps):
    count = lax.axis_size("context")
    rows, length = query_proj.shape
    taps = jnp.broadcast_to(filter_taps[:, None, :], (FILT, 1, length))
    taps = lax.all_to_all(taps, "tensor", 0, 0, tiled=True)
    rim = edge(key_proj, value_proj, query_proj)
    rim = lax.ppermute(rim, "context", [(n, n + 1) for n in range(count - 1)])
    weight = short_weight.reshape(9, rows)
    skip = skip_bias[None, :]
    outs = [((4, rows, TILE), jnp.float32), ((count, TILE), jnp.float32)]
    coded, scales = whole_call(
        front_kernel, "front", outs, key_proj, value_proj, weight, skip, rim
    )
    outs = [((count, CHUNK, TILE), jnp.bfloat16)]
    (chunks,) = whole_call(deal_kernel, "deal", outs, coded, scales, taps)
    chunks = lax.all_to_all(chunks, "context", 0, 0, tiled=True)
    streams = (query_proj, key_proj, value_proj)
    chunks, query_short, base = conv(chunks, streams, weight, skip, rim)
    chunks = lax.all_to_all(chunks, "context", 0, 0, tiled=True)
    return back(chunks, query_short, base)


def solution(mesh):
    in_specs = (
        P("tensor", "context"),
        P("tensor", "context"),
        P("tensor", "context"),
        P(None, None, "tensor"),
        P("tensor"),
        P("tensor", "context"),
    )
    out_specs = P("tensor", "context")
    return jax.shard_map(local, mesh=mesh, in_specs=in_specs, out_specs=out_specs, check_vma=False)
```

```python
import jax
import jax.numpy as jnp
from jax import lax
from jax.experimental import pallas as pl
from jax.experimental.pallas import tpu as pltpu
from jax.sharding import PartitionSpec as P

FILT = 8
TILE = 128
ROWS = 16
CHUNK = 72
GAIN = 16.0
SLOPE = 61.0
LIFT = 125.0
TINY = 1e-30
MIB = 1024 * 1024


def scale_of(peak):
    return jnp.maximum(peak, TINY).astype(jnp.bfloat16).astype(jnp.float32)


def encode(values, scale):
    level = jnp.log2(1.0 + jnp.abs(values) * (GAIN / scale))
    size = jnp.exp2(level * SLOPE - LIFT)
    return jnp.where(values < 0.0, -size, size)


def decode(codes, scale):
    level = (jnp.log2(jnp.abs(codes)) + LIFT) * (1.0 / SLOPE)
    size = (jnp.exp2(level) - 1.0) * (scale * (1.0 / GAIN))
    return jnp.where(codes < 0.0, -size, size)


def split(values):
    high = values.astype(jnp.bfloat16)
    low = (values - high.astype(jnp.float32)).astype(jnp.bfloat16)
    return high, low


def short_mix(stream, weights):
    one = pltpu.roll(stream, 1, 1)
    two = pltpu.roll(stream, 2, 1)
    return weights[0] * stream + weights[1] * one + weights[2] * two


def to_lanes(column):
    shape = (TILE, TILE)
    lane = lax.broadcasted_iota(jnp.int32, shape, 1)
    group = lax.broadcasted_iota(jnp.int32, shape, 0) // FILT
    spread = jnp.where(lane == group, column, 0.0)
    return spread.reshape(ROWS, FILT, TILE).sum(axis=0)


def side_columns(rows):
    missing = 16 - sum(part.shape[0] for part in rows)
    rows = rows + [jnp.zeros((missing, TILE), jnp.float32)]
    return jnp.transpose(jnp.concatenate(rows, axis=0))


def product_of(key_ref, value_ref, side, rows):
    key = key_ref[rows, :].astype(jnp.float32)
    value = value_ref[rows, :].astype(jnp.float32)
    key_short = short_mix(key, [side[:, n : n + 1] for n in range(3, 6)])
    value_short = short_mix(value, [side[:, n : n + 1] for n in range(6, 9)])
    return key_short * value_short


def ends_of(refs, start):
    shape = (TILE, TILE)
    lane = lax.broadcasted_iota(jnp.int32, shape, 1)
    place = lax.broadcasted_iota(jnp.int32, shape, 0)
    total = None
    for index, ref in enumerate(refs):
        pick = (lane // 32 == index) & (place == start % TILE + lane % 32 // 16)
        part = jnp.dot(
            ref[:, start // TILE * TILE : start // TILE * TILE + TILE],
            pick.astype(jnp.bfloat16),
            preferred_element_type=jnp.float32,
        )
        total = part if total is None else total + part
    return total


def front_kernel(key_ref, value_ref, query_ref, weight_ref, coded_ref, scale_ref, ends_ref):
    length = key_ref.shape[1]
    refs = (key_ref, value_ref, query_ref)
    group = lax.broadcasted_iota(jnp.int32, (TILE, TILE), 0) // FILT
    own = lax.broadcasted_iota(jnp.int32, (TILE, TILE), 1) % ROWS == group
    lane = lax.broadcasted_iota(jnp.int32, (TILE, length), 1)
    both = [ends_of(refs, 0), ends_of(refs, length - 2)]
    for step in range(key_ref.shape[0] // TILE):
        rows = slice(step * TILE, (step + 1) * TILE)
        dests = slice(step * FILT, (step + 1) * FILT)
        for which in range(2):
            spread = jnp.where(own, both[which][rows, :], 0.0)
            ends_ref[which, dests, :] = spread.reshape(ROWS, FILT, TILE).sum(axis=0)
        side = side_columns([weight_ref[:, rows]])
        product = jnp.where(lane < 2, 0.0, product_of(key_ref, value_ref, side, rows))
        scale = scale_of(jnp.max(jnp.abs(product), axis=1, keepdims=True))
        coded_rows = encode(product, scale)
        for block in range(4):
            coded_ref[block, rows, :] = coded_rows[:, block * TILE : (block + 1) * TILE]
        scale_ref[dests, :] = to_lanes(scale)


def deal_kernel(coded_ref, scale_ref, ends_ref, taps_ref, out_ref):
    row = lax.broadcasted_iota(jnp.int32, (8, TILE), 0)
    tails = []
    for filt in range(FILT):
        taps = taps_ref[filt]
        tap_scale = scale_of(jnp.max(jnp.abs(taps)))
        tail = jnp.where(row == 5, tap_scale, 0.0)
        codes = encode(taps, tap_scale)
        for block in range(4):
            part = codes[:, block * TILE : (block + 1) * TILE]
            tail = jnp.where(row == block, part, tail)
        tails.append(tail)
    for dest in range(out_ref.shape[0]):
        step, filt = dest // FILT, dest % FILT
        for block in range(4):
            rows = pl.ds(step * TILE + filt, ROWS, stride=FILT)
            part = coded_ref[block, rows, :]
            out_ref[dest, block * ROWS : (block + 1) * ROWS, :] = part.astype(jnp.bfloat16)
        tail = jnp.where(row == 4, scale_ref[dest : dest + 1, :], tails[filt])
        tail = jnp.where(row == 6, ends_ref[0, dest : dest + 1, :], tail)
        tail = jnp.where(row == 7, ends_ref[1, dest : dest + 1, :], tail)
        out_ref[dest, 64:72, :] = tail.astype(jnp.bfloat16)


def gate_rows(streams, side, rows, local, query_out, base_out):
    query_ref, key_ref, value_ref = streams
    side = side[local, :]
    query = query_ref[rows, :].astype(jnp.float32)
    query_short = short_mix(query, [side[:, n : n + 1] for n in range(3)])
    query_out[rows, :] = query_short
    product = product_of(key_ref, value_ref, side, rows)
    base_out[rows, :] = query_short * (side[:, 9:10] * product)


FINE = 512.0
GATE_FROM = 2
GATE_STEP = 2
EARLY = 12
PER_STEP = 3


def unit_of(peak):
    power = jnp.exp2(7.0 - jnp.ceil(jnp.log2(jnp.maximum(peak, TINY))))
    return power.astype(jnp.bfloat16).astype(jnp.float32)


def four_parts(values):
    coarse = values.astype(jnp.bfloat16)
    wide = coarse.astype(jnp.float32)
    narrow = wide.astype(jnp.float8_e4m3fn)
    fine = ((values - wide) * FINE).astype(jnp.float8_e4m3fn)
    return coarse, narrow, fine


def own_weights(weight_ref, skip_ref):
    index = lax.axis_index("context")
    cols = pl.ds(pl.multiple_of(index // FILT * TILE, TILE), TILE)
    source = lax.broadcasted_iota(jnp.int32, (TILE, TILE), 0)
    lane = lax.broadcasted_iota(jnp.int32, (TILE, TILE), 1)
    pick = (source % FILT == index % FILT) & (source // FILT == lane % ROWS)
    zeros = jnp.zeros((6, TILE), jnp.float32)
    rows = jnp.concatenate([weight_ref[:, cols], skip_ref[:, cols], zeros], axis=0)
    return jnp.dot(
        rows,
        pick.astype(jnp.float32),
        precision=lax.Precision.HIGHEST,
        preferred_element_type=jnp.float32,
    )


def start_mix(first, before, weights):
    lane = lax.broadcasted_iota(jnp.int32, first.shape, 1)
    taps = []
    for lag in range(3):
        query, key, value = [weights[3 * n + lag : 3 * n + lag + 1, :] for n in range(3)]
        taps.append(jnp.where(lane < 32, key, jnp.where(lane < 64, value, query)))
    second = lane % 32 >= ROWS
    one = jnp.where(second, pltpu.roll(first, ROWS, 1), pltpu.roll(before, TILE - ROWS, 1))
    return taps[0] * first + taps[1] * one + taps[2] * before, weights[9:10, :]


def conv_kernel(
    in_ref,
    query_ref,
    key_ref,
    value_ref,
    weight_ref,
    skip_ref,
    out_ref,
    query_out,
    base_out,
    main,
    cross,
    taps,
    toep,
    toep_narrow,
    toep_fine,
    total,
    back_unit,
    first,
    last,
    start_prod,
    start_gate,
    start_base,
):
    streams = (query_ref, key_ref, value_ref)
    count = in_ref.shape[0]
    blocks = count * 2
    size = blocks * ROWS
    lane = lax.broadcasted_iota(jnp.int32, (ROWS, TILE), 1)
    row = lax.broadcasted_iota(jnp.int32, (ROWS, TILE), 0)
    diagonal = lane == row
    beside = lane == row + ROWS
    tail_row = lax.broadcasted_iota(jnp.int32, (8, TILE), 0)
    wide_lane = lax.broadcasted_iota(jnp.int32, (TILE, TILE), 1)
    causal = wide_lane >= lax.broadcasted_iota(jnp.int32, (TILE, TILE), 0)

    def tail_of(src):
        return in_ref[src, pl.ds(64, 8), :].astype(jnp.float32)

    last[0:1, :] = jnp.zeros((1, TILE), jnp.float32)
    peaks = None
    for src in range(count):
        tail = tail_of(src)
        peaks = tail if peaks is None else jnp.maximum(peaks, tail)
        taps[src * 4 : (src + 1) * 4, :] = decode(tail[0:4, :], tail[5:6, :])
        first[src : src + 1, :] = tail[6:7, :]
        last[src + 1 : src + 2, :] = tail[7:8, :]
    lane_weights = own_weights(weight_ref, skip_ref)
    mixed, skip = start_mix(first[...], last[0:count, :], lane_weights)
    product = mixed * pltpu.roll(mixed, TILE - 32, 1)
    query = pltpu.roll(mixed, TILE - 64, 1)
    start_prod[...] = product
    start_gate[...] = query
    start_base[...] = query * (skip * product)

    def column(mask, line):
        return jnp.sum(jnp.where(mask, line, 0.0), axis=1, keepdims=True)

    start_peak = jnp.max(jnp.abs(product), axis=0, keepdims=True)
    start_peak = jnp.maximum(column(diagonal, start_peak), column(beside, start_peak))
    unit = unit_of(jnp.maximum(column(diagonal, peaks[4:5, :]), start_peak))
    tap_unit = unit_of(peaks[5:6, 0:1])
    back_unit[...] = jnp.broadcast_to(1.0 / (unit * tap_unit), (ROWS, TILE))

    def unpack(src):
        tail = tail_of(src)
        scale = column(diagonal, tail[4:5, :]) * unit
        starts = start_prod[src : src + 1, :]
        early = jnp.where(lane == 0, column(diagonal, starts), column(beside, starts)) * unit
        at = slice(src * 32, (src + 1) * 32)
        for half in range(2):
            pair = []
            for block in (half, half + 2):
                part = in_ref[src, pl.ds(block * ROWS, ROWS), :].astype(jnp.float32)
                values = decode(part, scale)
                pair.append(jnp.where(lane < 2, early, values) if block == 0 else values)
            coarse, narrow, fine = four_parts(jnp.concatenate(pair, axis=0))
            main[at, pl.ds(half * TILE, TILE)] = coarse
            cross[at, pl.ds(half * TILE, TILE)] = fine
            cross[at, pl.ds((half + 2) * TILE, TILE)] = narrow

    def rolled(tile):
        line = jnp.broadcast_to(taps[tile : tile + 1, :] * tap_unit, (TILE, TILE))
        return pltpu.roll(line, 0, 1, stride=1, stride_axis=0)

    def build(tile, before):
        here = rolled(tile)
        coarse, narrow, fine = four_parts(jnp.where(causal, here, before))
        toep[tile + 1] = coarse
        toep_narrow[tile + 1] = narrow
        toep_fine[tile + 1] = fine
        return here

    def weight(ref, lag):
        top = jnp.concatenate([ref[2 * lag + 1], ref[2 * lag + 2]], axis=1)
        bottom = jnp.concatenate([ref[2 * lag], ref[2 * lag + 1]], axis=1)
        return jnp.concatenate([top, bottom], axis=0)

    def pack(dst):
        parts = []
        for block in range(4):
            at = pl.ds(dst * 32 + (block // 2) * ROWS, ROWS)
            parts.append(total[at, pl.ds((block % 2) * TILE, TILE)])
        peak = jnp.maximum(
            jnp.maximum(jnp.abs(parts[0]), jnp.abs(parts[1])),
            jnp.maximum(jnp.abs(parts[2]), jnp.abs(parts[3])),
        )
        scale = scale_of(jnp.max(peak, axis=1, keepdims=True))
        for block in range(4):
            codes = encode(parts[block], scale).astype(jnp.bfloat16)
            out_ref[dst, pl.ds(block * ROWS, ROWS), :] = codes
        sent = jnp.where(diagonal, scale * back_unit[...], 0.0)
        spread = jnp.sum(sent, axis=0, keepdims=True)
        plain = parts[0] * back_unit[...]
        long = jnp.where(diagonal, plain[:, 0:1], jnp.where(beside, plain[:, 1:2], 0.0))
        long = jnp.sum(long, axis=0, keepdims=True)
        ends = start_gate[dst : dst + 1, :] * long + start_base[dst : dst + 1, :]
        tail = jnp.where(tail_row == 0, spread, jnp.where(tail_row == 1, ends, 0.0))
        out_ref[dst, pl.ds(64, 8), :] = tail.astype(jnp.bfloat16)

    def lag_step(lag):
        rows = size - lag * ROWS
        part = jnp.dot(main[:rows, :], weight(toep, lag), preferred_element_type=jnp.float32)
        narrow = jnp.concatenate([weight(toep_narrow, lag), weight(toep_fine, lag)], axis=0)
        rest = jnp.dot(cross[:rows, :], narrow, preferred_element_type=jnp.float32)
        total[lag * ROWS :, :] += part + rest * (1.0 / FINE)

    def gate(piece, side):
        rows = slice(piece * 32, (piece + 1) * 32)
        local_rows = slice(piece % 4 * 32, piece % 4 * 32 + 32)
        gate_rows(streams, side, rows, local_rows, query_out, base_out)

    total[...] = jnp.zeros_like(total)
    toep[0] = jnp.zeros((TILE, TILE), toep.dtype)
    toep_narrow[0] = jnp.zeros((TILE, TILE), toep_narrow.dtype)
    toep_fine[0] = jnp.zeros((TILE, TILE), toep_fine.dtype)
    early = blocks * EARLY // 64
    ready = early // 2
    for src in range(ready):
        unpack(src)
    order = list(range(blocks - early, blocks)) + list(range(blocks - early))
    built = rolled(2 * order[0] - 1)
    built = build(2 * order[0] + 1, build(2 * order[0], build(2 * order[0] - 1, rolled(2 * order[0] - 2))))
    for index, lag in enumerate(order):
        if index + 1 < blocks:
            ahead = order[index + 1]
            if ahead == 0:
                built = jnp.zeros((TILE, TILE), jnp.float32)
            built = build(2 * ahead + 1, build(2 * ahead, built))
        lag_step(lag)
        while ready < min(count, early // 2 + (index + 1) * PER_STEP):
            unpack(ready)
            ready += 1
        place = index - early
        if place >= 0 and lag % 2 == 1:
            pack(lag // 2)
        if place >= GATE_FROM and (place - GATE_FROM) % GATE_STEP == 0:
            piece = (place - GATE_FROM) // GATE_STEP
            if piece < 16:
                if piece % 4 == 0:
                    cols = slice(piece * 32, piece * 32 + TILE)
                    side = side_columns([weight_ref[:, cols], skip_ref[:, cols]])
                gate(piece, side)
    for dst in range((blocks - early) // 2, count):
        pack(dst)


def conv(chunks, streams, weight, skip):
    count = chunks.shape[0]
    plane = jax.ShapeDtypeStruct(streams[0].shape, jnp.float32)
    size = count * 2 * ROWS
    tiles = (count * 4 + 1, TILE, TILE)
    whole = pl.BlockSpec(memory_space=pltpu.VMEM)
    return pl.pallas_call(
        conv_kernel,
        in_specs=[whole] * 6,
        out_specs=[whole] * 3,
        out_shape=[jax.ShapeDtypeStruct(chunks.shape, jnp.bfloat16), plane, plane],
        scratch_shapes=[
            pltpu.VMEM((size, 2 * TILE), jnp.bfloat16),
            pltpu.VMEM((size, 4 * TILE), jnp.float8_e4m3fn),
            pltpu.VMEM((count * 4, TILE), jnp.float32),
            pltpu.VMEM(tiles, jnp.bfloat16),
            pltpu.VMEM(tiles, jnp.float8_e4m3fn),
            pltpu.VMEM(tiles, jnp.float8_e4m3fn),
            pltpu.VMEM((size, 2 * TILE), jnp.float32),
            pltpu.VMEM((ROWS, TILE), jnp.float32),
            pltpu.VMEM((count, TILE), jnp.float32),
            pltpu.VMEM((count + 8, TILE), jnp.float32),
            pltpu.VMEM((count, TILE), jnp.float32),
            pltpu.VMEM((count, TILE), jnp.float32),
            pltpu.VMEM((count, TILE), jnp.float32),
        ],
        compiler_params=pltpu.CompilerParams(vmem_limit_bytes=24 * MIB),
        name="conv",
    )(chunks, *streams, weight, skip)


def back_kernel(in_ref, query_ref, base_ref, out_ref, plain, starts):
    lane = lax.broadcasted_iota(jnp.int32, (ROWS, TILE), 1)
    row = lax.broadcasted_iota(jnp.int32, (ROWS, TILE), 0)
    step = pl.program_id(0)
    for filt in range(FILT):
        src = step * FILT + filt
        tail = in_ref[src, pl.ds(64, 8), :].astype(jnp.float32)
        scale = jnp.sum(jnp.where(lane == row, tail[0:1, :], 0.0), axis=1, keepdims=True)
        zero = jnp.sum(jnp.where(lane == row, tail[1:2, :], 0.0), axis=1, keepdims=True)
        one = jnp.sum(jnp.where(lane == row + ROWS, tail[1:2, :], 0.0), axis=1, keepdims=True)
        starts[pl.ds(filt, ROWS, stride=FILT), :] = jnp.where(lane == 0, zero, one)
        for block in range(4):
            part = in_ref[src, pl.ds(block * ROWS, ROWS), :].astype(jnp.float32)
            plain[block, pl.ds(filt, ROWS, stride=FILT), :] = decode(part, scale)
    rows = pl.ds(pl.multiple_of(step * TILE, TILE), TILE)
    long = jnp.concatenate([plain[block] for block in range(4)], axis=1)
    mixed = query_ref[rows, :] * long + base_ref[rows, :]
    head = lax.broadcasted_iota(jnp.int32, (TILE, TILE), 1)
    out_ref[:, :TILE] = jnp.where(head < 2, starts[...], mixed[:, :TILE]).astype(jnp.bfloat16)
    out_ref[:, TILE:] = mixed[:, TILE:].astype(jnp.bfloat16)


WHOLE = pl.BlockSpec(memory_space=pltpu.VMEM)


def whole_call(kernel, name, outs, *operands):
    return pl.pallas_call(
        kernel,
        in_specs=[WHOLE] * len(operands),
        out_specs=[WHOLE] * len(outs),
        out_shape=[jax.ShapeDtypeStruct(shape, dtype) for shape, dtype in outs],
        compiler_params=pltpu.CompilerParams(vmem_limit_bytes=16 * MIB),
        name=name,
    )(*operands)


def back(chunks, query_short, base):
    rows, length = base.shape
    return pl.pallas_call(
        back_kernel,
        grid=(rows // TILE,),
        in_specs=[WHOLE] * 3,
        out_specs=pl.BlockSpec((TILE, length), lambda n: (n, 0)),
        out_shape=jax.ShapeDtypeStruct((rows, length), jnp.bfloat16),
        scratch_shapes=[
            pltpu.VMEM((4, TILE, TILE), jnp.float32),
            pltpu.VMEM((TILE, TILE), jnp.float32),
        ],
        compiler_params=pltpu.CompilerParams(vmem_limit_bytes=16 * MIB),
        name="back",
    )(chunks, query_short, base)


def local(query_proj, key_proj, value_proj, short_weight, skip_bias, filter_taps):
    count = lax.axis_size("context")
    rows, length = query_proj.shape
    taps = jnp.broadcast_to(filter_taps[:, None, :], (FILT, 1, length))
    taps = lax.all_to_all(taps, "tensor", 0, 0, tiled=True)
    weight = short_weight.reshape(9, rows)
    skip = skip_bias[None, :]
    outs = [
        ((4, rows, TILE), jnp.float32),
        ((count, TILE), jnp.float32),
        ((2, count, TILE), jnp.float32),
    ]
    streams = (key_proj, value_proj, query_proj)
    coded, scales, ends = whole_call(front_kernel, "front", outs, *streams, weight)
    outs = [((count, CHUNK, TILE), jnp.bfloat16)]
    (chunks,) = whole_call(deal_kernel, "deal", outs, coded, scales, ends, taps)
    chunks = lax.all_to_all(chunks, "context", 0, 0, tiled=True)
    streams = (query_proj, key_proj, value_proj)
    chunks, query_short, base = conv(chunks, streams, weight, skip)
    chunks = lax.all_to_all(chunks, "context", 0, 0, tiled=True)
    return back(chunks, query_short, base)


def solution(mesh):
    in_specs = (
        P("tensor", "context"),
        P("tensor", "context"),
        P("tensor", "context"),
        P(None, None, "tensor"),
        P("tensor"),
        P("tensor", "context"),
    )
    out_specs = P("tensor", "context")
    return jax.shard_map(local, mesh=mesh, in_specs=in_specs, out_specs=out_specs, check_vma=False)
```

```python
import jax
import jax.numpy as jnp
from jax import lax
from jax.experimental import pallas as pl
from jax.experimental.pallas import tpu as pltpu
from jax.sharding import PartitionSpec as P

FILT = 8
TILE = 128
ROWS = 16
CHUNK = 72
GAIN = 16.0
SLOPE = 61.0
LIFT = 125.0
TINY = 1e-30
MIB = 1024 * 1024


def scale_of(peak):
    return jnp.maximum(peak, TINY).astype(jnp.bfloat16).astype(jnp.float32)


def encode(values, scale):
    level = jnp.log2(1.0 + jnp.abs(values) * (GAIN / scale))
    size = jnp.exp2(level * SLOPE - LIFT)
    return jnp.where(values < 0.0, -size, size)


def decode(codes, scale):
    level = (jnp.log2(jnp.abs(codes)) + LIFT) * (1.0 / SLOPE)
    size = (jnp.exp2(level) - 1.0) * (scale * (1.0 / GAIN))
    return jnp.where(codes < 0.0, -size, size)


def split(values):
    high = values.astype(jnp.bfloat16)
    low = (values - high.astype(jnp.float32)).astype(jnp.bfloat16)
    return high, low


def short_mix(stream, weights):
    one = pltpu.roll(stream, 1, 1)
    two = pltpu.roll(stream, 2, 1)
    return weights[0] * stream + weights[1] * one + weights[2] * two


def to_lanes(column):
    shape = (TILE, TILE)
    lane = lax.broadcasted_iota(jnp.int32, shape, 1)
    group = lax.broadcasted_iota(jnp.int32, shape, 0) // FILT
    spread = jnp.where(lane == group, column, 0.0)
    return spread.reshape(ROWS, FILT, TILE).sum(axis=0)


def side_columns(rows):
    missing = 16 - sum(part.shape[0] for part in rows)
    rows = rows + [jnp.zeros((missing, TILE), jnp.float32)]
    return jnp.transpose(jnp.concatenate(rows, axis=0))


def product_of(key_ref, value_ref, side, rows):
    key = key_ref[rows, :].astype(jnp.float32)
    value = value_ref[rows, :].astype(jnp.float32)
    key_short = short_mix(key, [side[:, n : n + 1] for n in range(3, 6)])
    value_short = short_mix(value, [side[:, n : n + 1] for n in range(6, 9)])
    return key_short * value_short


def ends_of(refs, start):
    shape = (TILE, TILE)
    lane = lax.broadcasted_iota(jnp.int32, shape, 1)
    place = lax.broadcasted_iota(jnp.int32, shape, 0)
    total = None
    for index, ref in enumerate(refs):
        pick = (lane // 32 == index) & (place == start % TILE + lane % 32 // 16)
        part = jnp.dot(
            ref[:, start // TILE * TILE : start // TILE * TILE + TILE],
            pick.astype(jnp.bfloat16),
            preferred_element_type=jnp.float32,
        )
        total = part if total is None else total + part
    return total


def front_kernel(key_ref, value_ref, query_ref, weight_ref, coded_ref, scale_ref, ends_ref):
    length = key_ref.shape[1]
    refs = (key_ref, value_ref, query_ref)
    group = lax.broadcasted_iota(jnp.int32, (TILE, TILE), 0) // FILT
    own = lax.broadcasted_iota(jnp.int32, (TILE, TILE), 1) % ROWS == group
    lane = lax.broadcasted_iota(jnp.int32, (TILE, length), 1)
    both = [ends_of(refs, 0), ends_of(refs, length - 2)]
    for step in range(key_ref.shape[0] // TILE):
        rows = slice(step * TILE, (step + 1) * TILE)
        dests = slice(step * FILT, (step + 1) * FILT)
        for which in range(2):
            spread = jnp.where(own, both[which][rows, :], 0.0)
            ends_ref[which, dests, :] = spread.reshape(ROWS, FILT, TILE).sum(axis=0)
        side = side_columns([weight_ref[:, rows]])
        product = jnp.where(lane < 2, 0.0, product_of(key_ref, value_ref, side, rows))
        scale = scale_of(jnp.max(jnp.abs(product), axis=1, keepdims=True))
        coded_rows = encode(product, scale)
        for block in range(4):
            coded_ref[block, rows, :] = coded_rows[:, block * TILE : (block + 1) * TILE]
        scale_ref[dests, :] = to_lanes(scale)


def deal_kernel(coded_ref, scale_ref, ends_ref, taps_ref, out_ref):
    row = lax.broadcasted_iota(jnp.int32, (8, TILE), 0)
    tails = []
    for filt in range(FILT):
        taps = taps_ref[filt]
        tap_scale = scale_of(jnp.max(jnp.abs(taps)))
        tail = jnp.where(row == 5, tap_scale, 0.0)
        codes = encode(taps, tap_scale)
        for block in range(4):
            part = codes[:, block * TILE : (block + 1) * TILE]
            tail = jnp.where(row == block, part, tail)
        tails.append(tail)
    for dest in range(out_ref.shape[0]):
        step, filt = dest // FILT, dest % FILT
        for block in range(4):
            rows = pl.ds(step * TILE + filt, ROWS, stride=FILT)
            part = coded_ref[block, rows, :]
            out_ref[dest, block * ROWS : (block + 1) * ROWS, :] = part.astype(jnp.bfloat16)
        tail = jnp.where(row == 4, scale_ref[dest : dest + 1, :], tails[filt])
        tail = jnp.where(row == 6, ends_ref[0, dest : dest + 1, :], tail)
        tail = jnp.where(row == 7, ends_ref[1, dest : dest + 1, :], tail)
        out_ref[dest, 64:72, :] = tail.astype(jnp.bfloat16)


def gate_rows(streams, side, rows, local, query_out, base_out):
    query_ref, key_ref, value_ref = streams
    side = side[local, :]
    query = query_ref[rows, :].astype(jnp.float32)
    query_short = short_mix(query, [side[:, n : n + 1] for n in range(3)])
    query_out[rows, :] = query_short
    product = product_of(key_ref, value_ref, side, rows)
    base_out[rows, :] = query_short * (side[:, 9:10] * product)


FINE = 512.0
GATE_FROM = 0
GATE_STEP = 1
EARLY = 4
PER_STEP = 8


def unit_of(peak):
    power = jnp.exp2(7.0 - jnp.ceil(jnp.log2(jnp.maximum(peak, TINY))))
    return power.astype(jnp.bfloat16).astype(jnp.float32)


def four_parts(values):
    coarse = values.astype(jnp.bfloat16)
    wide = coarse.astype(jnp.float32)
    narrow = wide.astype(jnp.float8_e4m3fn)
    fine = ((values - wide) * FINE).astype(jnp.float8_e4m3fn)
    return coarse, narrow, fine


def own_weights(weight_ref, skip_ref):
    index = lax.axis_index("context")
    cols = pl.ds(pl.multiple_of(index // FILT * TILE, TILE), TILE)
    source = lax.broadcasted_iota(jnp.int32, (TILE, TILE), 0)
    lane = lax.broadcasted_iota(jnp.int32, (TILE, TILE), 1)
    pick = (source % FILT == index % FILT) & (source // FILT == lane % ROWS)
    zeros = jnp.zeros((6, TILE), jnp.float32)
    rows = jnp.concatenate([weight_ref[:, cols], skip_ref[:, cols], zeros], axis=0)
    return jnp.dot(
        rows,
        pick.astype(jnp.float32),
        precision=lax.Precision.HIGHEST,
        preferred_element_type=jnp.float32,
    )


def start_mix(first, before, weights):
    lane = lax.broadcasted_iota(jnp.int32, first.shape, 1)
    taps = []
    for lag in range(3):
        query, key, value = [weights[3 * n + lag : 3 * n + lag + 1, :] for n in range(3)]
        taps.append(jnp.where(lane < 32, key, jnp.where(lane < 64, value, query)))
    second = lane % 32 >= ROWS
    one = jnp.where(second, pltpu.roll(first, ROWS, 1), pltpu.roll(before, TILE - ROWS, 1))
    return taps[0] * first + taps[1] * one + taps[2] * before, weights[9:10, :]


def conv_kernel(
    in_ref,
    query_ref,
    key_ref,
    value_ref,
    weight_ref,
    skip_ref,
    out_ref,
    query_out,
    base_out,
    main,
    cross,
    taps,
    toep,
    toep_narrow,
    toep_fine,
    total,
    back_unit,
    first,
    last,
    start_prod,
    start_gate,
    start_base,
):
    streams = (query_ref, key_ref, value_ref)
    count = in_ref.shape[0]
    blocks = count * 2
    size = blocks * ROWS
    lane = lax.broadcasted_iota(jnp.int32, (ROWS, TILE), 1)
    row = lax.broadcasted_iota(jnp.int32, (ROWS, TILE), 0)
    diagonal = lane == row
    beside = lane == row + ROWS
    tail_row = lax.broadcasted_iota(jnp.int32, (8, TILE), 0)
    wide_lane = lax.broadcasted_iota(jnp.int32, (TILE, TILE), 1)
    causal = wide_lane >= lax.broadcasted_iota(jnp.int32, (TILE, TILE), 0)

    def tail_of(src):
        return in_ref[src, pl.ds(64, 8), :].astype(jnp.float32)

    last[0:1, :] = jnp.zeros((1, TILE), jnp.float32)
    peaks = None
    for src in range(count):
        tail = tail_of(src)
        peaks = tail if peaks is None else jnp.maximum(peaks, tail)
        taps[src * 4 : (src + 1) * 4, :] = decode(tail[0:4, :], tail[5:6, :])
        first[src : src + 1, :] = tail[6:7, :]
        last[src + 1 : src + 2, :] = tail[7:8, :]
    lane_weights = own_weights(weight_ref, skip_ref)
    mixed, skip = start_mix(first[...], last[0:count, :], lane_weights)
    product = mixed * pltpu.roll(mixed, TILE - 32, 1)
    query = pltpu.roll(mixed, TILE - 64, 1)
    start_prod[...] = product
    start_gate[...] = query
    start_base[...] = query * (skip * product)

    def column(mask, line):
        return jnp.sum(jnp.where(mask, line, 0.0), axis=1, keepdims=True)

    start_peak = jnp.max(jnp.abs(product), axis=0, keepdims=True)
    start_peak = jnp.maximum(column(diagonal, start_peak), column(beside, start_peak))
    unit = unit_of(jnp.maximum(column(diagonal, peaks[4:5, :]), start_peak))
    tap_unit = unit_of(peaks[5:6, 0:1])
    back_unit[...] = jnp.broadcast_to(1.0 / (unit * tap_unit), (ROWS, TILE))

    def unpack(src):
        tail = tail_of(src)
        scale = column(diagonal, tail[4:5, :]) * unit
        starts = start_prod[src : src + 1, :]
        early = jnp.where(lane == 0, column(diagonal, starts), column(beside, starts)) * unit
        at = slice(src * 32, (src + 1) * 32)
        for half in range(2):
            pair = []
            for block in (half, half + 2):
                part = in_ref[src, pl.ds(block * ROWS, ROWS), :].astype(jnp.float32)
                values = decode(part, scale)
                pair.append(jnp.where(lane < 2, early, values) if block == 0 else values)
            coarse, narrow, fine = four_parts(jnp.concatenate(pair, axis=0))
            main[at, pl.ds(half * TILE, TILE)] = coarse
            cross[at, pl.ds(half * TILE, TILE)] = fine
            cross[at, pl.ds((half + 2) * TILE, TILE)] = narrow

    def rolled(tile):
        line = jnp.broadcast_to(taps[tile : tile + 1, :] * tap_unit, (TILE, TILE))
        return pltpu.roll(line, 0, 1, stride=1, stride_axis=0)

    def build(tile, before):
        here = rolled(tile)
        coarse, narrow, fine = four_parts(jnp.where(causal, here, before))
        toep[tile + 1] = coarse
        toep_narrow[tile + 1] = narrow
        toep_fine[tile + 1] = fine
        return here

    def weight(ref, lag):
        top = jnp.concatenate([ref[2 * lag + 1], ref[2 * lag + 2]], axis=1)
        bottom = jnp.concatenate([ref[2 * lag], ref[2 * lag + 1]], axis=1)
        return jnp.concatenate([top, bottom], axis=0)

    def pack(dst):
        parts = []
        for block in range(4):
            at = pl.ds(dst * 32 + (block // 2) * ROWS, ROWS)
            parts.append(total[at, pl.ds((block % 2) * TILE, TILE)])
        peak = jnp.maximum(
            jnp.maximum(jnp.abs(parts[0]), jnp.abs(parts[1])),
            jnp.maximum(jnp.abs(parts[2]), jnp.abs(parts[3])),
        )
        scale = scale_of(jnp.max(peak, axis=1, keepdims=True))
        for block in range(4):
            codes = encode(parts[block], scale).astype(jnp.bfloat16)
            out_ref[dst, pl.ds(block * ROWS, ROWS), :] = codes
        sent = jnp.where(diagonal, scale * back_unit[...], 0.0)
        spread = jnp.sum(sent, axis=0, keepdims=True)
        plain = parts[0] * back_unit[...]
        long = jnp.where(diagonal, plain[:, 0:1], jnp.where(beside, plain[:, 1:2], 0.0))
        long = jnp.sum(long, axis=0, keepdims=True)
        ends = start_gate[dst : dst + 1, :] * long + start_base[dst : dst + 1, :]
        tail = jnp.where(tail_row == 0, spread, jnp.where(tail_row == 1, ends, 0.0))
        out_ref[dst, pl.ds(64, 8), :] = tail.astype(jnp.bfloat16)

    def lag_step(lag):
        rows = size - lag * ROWS
        part = jnp.dot(main[:rows, :], weight(toep, lag), preferred_element_type=jnp.float32)
        narrow = jnp.concatenate([weight(toep_narrow, lag), weight(toep_fine, lag)], axis=0)
        rest = jnp.dot(cross[:rows, :], narrow, preferred_element_type=jnp.float32)
        total[lag * ROWS :, :] += part + rest * (1.0 / FINE)

    def gate(piece, side):
        rows = slice(piece * 32, (piece + 1) * 32)
        local_rows = slice(piece % 4 * 32, piece % 4 * 32 + 32)
        gate_rows(streams, side, rows, local_rows, query_out, base_out)

    total[...] = jnp.zeros_like(total)
    toep[0] = jnp.zeros((TILE, TILE), toep.dtype)
    toep_narrow[0] = jnp.zeros((TILE, TILE), toep_narrow.dtype)
    toep_fine[0] = jnp.zeros((TILE, TILE), toep_fine.dtype)
    early = blocks * EARLY // 64
    ready = early // 2
    for src in range(ready):
        unpack(src)
    order = list(range(blocks - early, blocks)) + list(range(blocks - early))
    built = rolled(2 * order[0] - 1)
    built = build(2 * order[0] + 1, build(2 * order[0], build(2 * order[0] - 1, rolled(2 * order[0] - 2))))
    for index, lag in enumerate(order):
        if index + 1 < blocks:
            ahead = order[index + 1]
            if ahead == 0:
                built = jnp.zeros((TILE, TILE), jnp.float32)
            built = build(2 * ahead + 1, build(2 * ahead, built))
        lag_step(lag)
        while ready < min(count, early // 2 + (index + 1) * PER_STEP):
            unpack(ready)
            ready += 1
        place = index - early
        if place >= 0 and lag % 2 == 1:
            pack(lag // 2)
        if place >= GATE_FROM and (place - GATE_FROM) % GATE_STEP == 0:
            piece = (place - GATE_FROM) // GATE_STEP
            if piece < 16:
                if piece % 4 == 0:
                    cols = slice(piece * 32, piece * 32 + TILE)
                    side = side_columns([weight_ref[:, cols], skip_ref[:, cols]])
                gate(piece, side)
    for dst in range((blocks - early) // 2, count):
        pack(dst)


def conv(chunks, streams, weight, skip):
    count = chunks.shape[0]
    plane = jax.ShapeDtypeStruct(streams[0].shape, jnp.float32)
    size = count * 2 * ROWS
    tiles = (count * 4 + 1, TILE, TILE)
    whole = pl.BlockSpec(memory_space=pltpu.VMEM)
    return pl.pallas_call(
        conv_kernel,
        in_specs=[whole] * 6,
        out_specs=[whole] * 3,
        out_shape=[jax.ShapeDtypeStruct(chunks.shape, jnp.bfloat16), plane, plane],
        scratch_shapes=[
            pltpu.VMEM((size, 2 * TILE), jnp.bfloat16),
            pltpu.VMEM((size, 4 * TILE), jnp.float8_e4m3fn),
            pltpu.VMEM((count * 4, TILE), jnp.float32),
            pltpu.VMEM(tiles, jnp.bfloat16),
            pltpu.VMEM(tiles, jnp.float8_e4m3fn),
            pltpu.VMEM(tiles, jnp.float8_e4m3fn),
            pltpu.VMEM((size, 2 * TILE), jnp.float32),
            pltpu.VMEM((ROWS, TILE), jnp.float32),
            pltpu.VMEM((count, TILE), jnp.float32),
            pltpu.VMEM((count + 8, TILE), jnp.float32),
            pltpu.VMEM((count, TILE), jnp.float32),
            pltpu.VMEM((count, TILE), jnp.float32),
            pltpu.VMEM((count, TILE), jnp.float32),
        ],
        compiler_params=pltpu.CompilerParams(vmem_limit_bytes=24 * MIB),
        name="conv",
    )(chunks, *streams, weight, skip)


def back_kernel(in_ref, query_ref, base_ref, out_hbm, plain, starts, done, sent):
    lane = lax.broadcasted_iota(jnp.int32, (ROWS, TILE), 1)
    row = lax.broadcasted_iota(jnp.int32, (ROWS, TILE), 0)
    head = lax.broadcasted_iota(jnp.int32, (TILE, TILE), 1)
    copies = []
    for step in range(done.shape[0] // TILE):
        for filt in range(FILT):
            src = step * FILT + filt
            tail = in_ref[src, pl.ds(64, 8), :].astype(jnp.float32)
            scale = jnp.sum(jnp.where(lane == row, tail[0:1, :], 0.0), axis=1, keepdims=True)
            zero = jnp.sum(jnp.where(lane == row, tail[1:2, :], 0.0), axis=1, keepdims=True)
            one = jnp.where(lane == row + ROWS, tail[1:2, :], 0.0)
            one = jnp.sum(one, axis=1, keepdims=True)
            starts[step, pl.ds(filt, ROWS, stride=FILT), :] = jnp.where(lane == 0, zero, one)
            for block in range(4):
                part = in_ref[src, pl.ds(block * ROWS, ROWS), :].astype(jnp.float32)
                plain[step, block, pl.ds(filt, ROWS, stride=FILT), :] = decode(part, scale)
        rows = pl.ds(step * TILE, TILE)
        for block in range(4):
            cols = pl.ds(block * TILE, TILE)
            mixed = query_ref[rows, cols] * plain[step, block] + base_ref[rows, cols]
            if block == 0:
                mixed = jnp.where(head < 2, starts[step], mixed)
            done[rows, cols] = mixed.astype(jnp.bfloat16)
        copy = pltpu.make_async_copy(done.at[rows, :], out_hbm.at[rows, :], sent.at[step])
        copy.start()
        copies.append(copy)
    for copy in copies:
        copy.wait()


WHOLE = pl.BlockSpec(memory_space=pltpu.VMEM)


def whole_call(kernel, name, outs, *operands):
    return pl.pallas_call(
        kernel,
        in_specs=[WHOLE] * len(operands),
        out_specs=[WHOLE] * len(outs),
        out_shape=[jax.ShapeDtypeStruct(shape, dtype) for shape, dtype in outs],
        compiler_params=pltpu.CompilerParams(vmem_limit_bytes=16 * MIB),
        name=name,
    )(*operands)


def back(chunks, query_short, base):
    rows, length = base.shape
    steps = rows // TILE
    return pl.pallas_call(
        back_kernel,
        in_specs=[WHOLE] * 3,
        out_specs=pl.BlockSpec(memory_space=pl.ANY),
        out_shape=jax.ShapeDtypeStruct((rows, length), jnp.bfloat16),
        scratch_shapes=[
            pltpu.VMEM((steps, 4, TILE, TILE), jnp.float32),
            pltpu.VMEM((steps, TILE, TILE), jnp.float32),
            pltpu.VMEM((rows, length), jnp.bfloat16),
            pltpu.SemaphoreType.DMA((steps,)),
        ],
        compiler_params=pltpu.CompilerParams(vmem_limit_bytes=16 * MIB),
        name="back",
    )(chunks, query_short, base)


def local(query_proj, key_proj, value_proj, short_weight, skip_bias, filter_taps):
    count = lax.axis_size("context")
    rows, length = query_proj.shape
    taps = jnp.broadcast_to(filter_taps[:, None, :], (FILT, 1, length))
    taps = lax.all_to_all(taps, "tensor", 0, 0, tiled=True)
    weight = short_weight.reshape(9, rows)
    skip = skip_bias[None, :]
    outs = [
        ((4, rows, TILE), jnp.float32),
        ((count, TILE), jnp.float32),
        ((2, count, TILE), jnp.float32),
    ]
    streams = (key_proj, value_proj, query_proj)
    coded, scales, ends = whole_call(front_kernel, "front", outs, *streams, weight)
    outs = [((count, CHUNK, TILE), jnp.bfloat16)]
    (chunks,) = whole_call(deal_kernel, "deal", outs, coded, scales, ends, taps)
    chunks = lax.all_to_all(chunks, "context", 0, 0, tiled=True)
    streams = (query_proj, key_proj, value_proj)
    chunks, query_short, base = conv(chunks, streams, weight, skip)
    chunks = lax.all_to_all(chunks, "context", 0, 0, tiled=True)
    return back(chunks, query_short, base)


def solution(mesh):
    in_specs = (
        P("tensor", "context"),
        P("tensor", "context"),
        P("tensor", "context"),
        P(None, None, "tensor"),
        P("tensor"),
        P("tensor", "context"),
    )
    out_specs = P("tensor", "context")
    return jax.shard_map(local, mesh=mesh, in_specs=in_specs, out_specs=out_specs, check_vma=False)
```

```python
import jax
import jax.numpy as jnp
from jax import lax
from jax.experimental import pallas as pl
from jax.experimental.pallas import tpu as pltpu
from jax.sharding import PartitionSpec as P

FILT = 8
TILE = 128
ROWS = 16
CHUNK = 72
GAIN = 16.0
SLOPE = 61.0
LIFT = 125.0
TINY = 1e-30
MIB = 1024 * 1024


def scale_of(peak):
    return jnp.maximum(peak, TINY).astype(jnp.bfloat16).astype(jnp.float32)


def encode(values, scale):
    level = jnp.log2(1.0 + jnp.abs(values) * (GAIN / scale))
    size = jnp.exp2(level * SLOPE - LIFT)
    return jnp.where(values < 0.0, -size, size)


def decode(codes, scale):
    level = (jnp.log2(jnp.abs(codes)) + LIFT) * (1.0 / SLOPE)
    size = (jnp.exp2(level) - 1.0) * (scale * (1.0 / GAIN))
    return jnp.where(codes < 0.0, -size, size)


def split(values):
    high = values.astype(jnp.bfloat16)
    low = (values - high.astype(jnp.float32)).astype(jnp.bfloat16)
    return high, low


def short_mix(stream, weights):
    one = pltpu.roll(stream, 1, 1)
    two = pltpu.roll(stream, 2, 1)
    return weights[0] * stream + weights[1] * one + weights[2] * two


def to_lanes(column):
    shape = (TILE, TILE)
    lane = lax.broadcasted_iota(jnp.int32, shape, 1)
    group = lax.broadcasted_iota(jnp.int32, shape, 0) // FILT
    spread = jnp.where(lane == group, column, 0.0)
    return spread.reshape(ROWS, FILT, TILE).sum(axis=0)


def side_columns(rows):
    missing = 16 - sum(part.shape[0] for part in rows)
    rows = rows + [jnp.zeros((missing, TILE), jnp.float32)]
    return jnp.transpose(jnp.concatenate(rows, axis=0))


def product_of(key_ref, value_ref, side, rows):
    key = key_ref[rows, :].astype(jnp.float32)
    value = value_ref[rows, :].astype(jnp.float32)
    key_short = short_mix(key, [side[:, n : n + 1] for n in range(3, 6)])
    value_short = short_mix(value, [side[:, n : n + 1] for n in range(6, 9)])
    return key_short * value_short


def ends_of(refs, start, base):
    shape = (TILE, TILE)
    lane = lax.broadcasted_iota(jnp.int32, shape, 1)
    place = lax.broadcasted_iota(jnp.int32, shape, 0)
    total = None
    for index, ref in enumerate(refs):
        pick = (lane // 32 == base + index) & (place == start % TILE + lane % 32 // 16)
        part = jnp.dot(
            ref[:, start // TILE * TILE : start // TILE * TILE + TILE],
            pick.astype(jnp.bfloat16),
            preferred_element_type=jnp.float32,
        )
        total = part if total is None else total + part
    return total


def ends_rows(both, step):
    group = lax.broadcasted_iota(jnp.int32, (TILE, TILE), 0) // FILT
    own = lax.broadcasted_iota(jnp.int32, (TILE, TILE), 1) % ROWS == group
    rows = slice(step * TILE, (step + 1) * TILE)
    spread = [jnp.where(own, part[rows, :], 0.0) for part in both]
    return [part.reshape(ROWS, FILT, TILE).sum(axis=0) for part in spread]


def front_kernel(key_ref, value_ref, weight_ref, coded_ref, scale_ref, ends_ref):
    length = key_ref.shape[1]
    refs = (key_ref, value_ref)
    lane = lax.broadcasted_iota(jnp.int32, (TILE, length), 1)
    both = [ends_of(refs, start, 0) for start in (0, length - 2)]
    for step in range(key_ref.shape[0] // TILE):
        rows = slice(step * TILE, (step + 1) * TILE)
        dests = slice(step * FILT, (step + 1) * FILT)
        for which, part in enumerate(ends_rows(both, step)):
            ends_ref[which, dests, :] = part
        side = side_columns([weight_ref[:, rows]])
        product = jnp.where(lane < 2, 0.0, product_of(key_ref, value_ref, side, rows))
        scale = scale_of(jnp.max(jnp.abs(product), axis=1, keepdims=True))
        coded_rows = encode(product, scale)
        for block in range(4):
            coded_ref[block, rows, :] = coded_rows[:, block * TILE : (block + 1) * TILE]
        scale_ref[dests, :] = to_lanes(scale)


def deal_kernel(coded_ref, scale_ref, ends_ref, query_ref, taps_ref, out_ref):
    both = [ends_of((query_ref,), start, 2) for start in (0, query_ref.shape[1] - 2)]
    row = lax.broadcasted_iota(jnp.int32, (8, TILE), 0)
    tails = []
    for filt in range(FILT):
        taps = taps_ref[filt]
        tap_scale = scale_of(jnp.max(jnp.abs(taps)))
        tail = jnp.where(row == 5, tap_scale, 0.0)
        codes = encode(taps, tap_scale)
        for block in range(4):
            part = codes[:, block * TILE : (block + 1) * TILE]
            tail = jnp.where(row == block, part, tail)
        tails.append(tail)
    for dest in range(out_ref.shape[0]):
        step, filt = dest // FILT, dest % FILT
        if filt == 0:
            late = ends_rows(both, step)
        for block in range(4):
            rows = pl.ds(step * TILE + filt, ROWS, stride=FILT)
            part = coded_ref[block, rows, :]
            out_ref[dest, block * ROWS : (block + 1) * ROWS, :] = part.astype(jnp.bfloat16)
        tail = jnp.where(row == 4, scale_ref[dest : dest + 1, :], tails[filt])
        ends = ends_ref[0, dest : dest + 1, :] + late[0][filt : filt + 1, :]
        tail = jnp.where(row == 6, ends, tail)
        ends = ends_ref[1, dest : dest + 1, :] + late[1][filt : filt + 1, :]
        tail = jnp.where(row == 7, ends, tail)
        out_ref[dest, 64:72, :] = tail.astype(jnp.bfloat16)


def gate_rows(streams, side, rows, local, query_out, base_out):
    query_ref, key_ref, value_ref = streams
    side = side[local, :]
    query = query_ref[rows, :].astype(jnp.float32)
    query_short = short_mix(query, [side[:, n : n + 1] for n in range(3)])
    query_out[rows, :] = query_short
    product = product_of(key_ref, value_ref, side, rows)
    base_out[rows, :] = query_short * (side[:, 9:10] * product)


FINE = 512.0
GATE_FROM = 0
GATE_STEP = 1
EARLY = 4
PER_STEP = 8


def unit_of(peak):
    power = jnp.exp2(7.0 - jnp.ceil(jnp.log2(jnp.maximum(peak, TINY))))
    return power.astype(jnp.bfloat16).astype(jnp.float32)


def four_parts(values):
    coarse = values.astype(jnp.bfloat16)
    wide = coarse.astype(jnp.float32)
    narrow = wide.astype(jnp.float8_e4m3fn)
    fine = ((values - wide) * FINE).astype(jnp.float8_e4m3fn)
    return coarse, narrow, fine


def own_weights(weight_ref, skip_ref):
    index = lax.axis_index("context")
    cols = pl.ds(pl.multiple_of(index // FILT * TILE, TILE), TILE)
    source = lax.broadcasted_iota(jnp.int32, (TILE, TILE), 0)
    lane = lax.broadcasted_iota(jnp.int32, (TILE, TILE), 1)
    pick = (source % FILT == index % FILT) & (source // FILT == lane % ROWS)
    zeros = jnp.zeros((6, TILE), jnp.float32)
    rows = jnp.concatenate([weight_ref[:, cols], skip_ref[:, cols], zeros], axis=0)
    return jnp.dot(
        rows,
        pick.astype(jnp.float32),
        precision=lax.Precision.HIGHEST,
        preferred_element_type=jnp.float32,
    )


def start_mix(first, before, weights):
    lane = lax.broadcasted_iota(jnp.int32, first.shape, 1)
    taps = []
    for lag in range(3):
        query, key, value = [weights[3 * n + lag : 3 * n + lag + 1, :] for n in range(3)]
        taps.append(jnp.where(lane < 32, key, jnp.where(lane < 64, value, query)))
    second = lane % 32 >= ROWS
    one = jnp.where(second, pltpu.roll(first, ROWS, 1), pltpu.roll(before, TILE - ROWS, 1))
    return taps[0] * first + taps[1] * one + taps[2] * before, weights[9:10, :]


def conv_kernel(
    in_ref,
    query_ref,
    key_ref,
    value_ref,
    weight_ref,
    skip_ref,
    out_ref,
    query_out,
    base_out,
    main,
    cross,
    taps,
    toep,
    toep_narrow,
    toep_fine,
    total,
    back_unit,
    first,
    last,
    start_prod,
    start_gate,
    start_base,
):
    streams = (query_ref, key_ref, value_ref)
    count = in_ref.shape[0]
    blocks = count * 2
    size = blocks * ROWS
    lane = lax.broadcasted_iota(jnp.int32, (ROWS, TILE), 1)
    row = lax.broadcasted_iota(jnp.int32, (ROWS, TILE), 0)
    diagonal = lane == row
    beside = lane == row + ROWS
    tail_row = lax.broadcasted_iota(jnp.int32, (8, TILE), 0)
    wide_lane = lax.broadcasted_iota(jnp.int32, (TILE, TILE), 1)
    causal = wide_lane >= lax.broadcasted_iota(jnp.int32, (TILE, TILE), 0)

    def tail_of(src):
        return in_ref[src, pl.ds(64, 8), :].astype(jnp.float32)

    last[0:1, :] = jnp.zeros((1, TILE), jnp.float32)
    peaks = None
    for src in range(count):
        tail = tail_of(src)
        peaks = tail if peaks is None else jnp.maximum(peaks, tail)
        taps[src * 4 : (src + 1) * 4, :] = decode(tail[0:4, :], tail[5:6, :])
        first[src : src + 1, :] = tail[6:7, :]
        last[src + 1 : src + 2, :] = tail[7:8, :]
    lane_weights = own_weights(weight_ref, skip_ref)
    mixed, skip = start_mix(first[...], last[0:count, :], lane_weights)
    product = mixed * pltpu.roll(mixed, TILE - 32, 1)
    query = pltpu.roll(mixed, TILE - 64, 1)
    start_prod[...] = product
    start_gate[...] = query
    start_base[...] = query * (skip * product)

    def column(mask, line):
        return jnp.sum(jnp.where(mask, line, 0.0), axis=1, keepdims=True)

    start_peak = jnp.max(jnp.abs(product), axis=0, keepdims=True)
    start_peak = jnp.maximum(column(diagonal, start_peak), column(beside, start_peak))
    unit = unit_of(jnp.maximum(column(diagonal, peaks[4:5, :]), start_peak))
    tap_unit = unit_of(peaks[5:6, 0:1])
    back_unit[...] = jnp.broadcast_to(1.0 / (unit * tap_unit), (ROWS, TILE))

    def unpack(src):
        tail = tail_of(src)
        scale = column(diagonal, tail[4:5, :]) * unit
        starts = start_prod[src : src + 1, :]
        early = jnp.where(lane == 0, column(diagonal, starts), column(beside, starts)) * unit
        at = slice(src * 32, (src + 1) * 32)
        for half in range(2):
            pair = []
            for block in (half, half + 2):
                part = in_ref[src, pl.ds(block * ROWS, ROWS), :].astype(jnp.float32)
                values = decode(part, scale)
                pair.append(jnp.where(lane < 2, early, values) if block == 0 else values)
            coarse, narrow, fine = four_parts(jnp.concatenate(pair, axis=0))
            main[at, pl.ds(half * TILE, TILE)] = coarse
            cross[at, pl.ds(half * TILE, TILE)] = fine
            cross[at, pl.ds((half + 2) * TILE, TILE)] = narrow

    def rolled(tile):
        line = jnp.broadcast_to(taps[tile : tile + 1, :] * tap_unit, (TILE, TILE))
        return pltpu.roll(line, 0, 1, stride=1, stride_axis=0)

    def build(tile, before):
        here = rolled(tile)
        coarse, narrow, fine = four_parts(jnp.where(causal, here, before))
        toep[tile + 1] = coarse
        toep_narrow[tile + 1] = narrow
        toep_fine[tile + 1] = fine
        return here

    def weight(ref, lag):
        top = jnp.concatenate([ref[2 * lag + 1], ref[2 * lag + 2]], axis=1)
        bottom = jnp.concatenate([ref[2 * lag], ref[2 * lag + 1]], axis=1)
        return jnp.concatenate([top, bottom], axis=0)

    def pack(dst):
        parts = []
        for block in range(4):
            at = pl.ds(dst * 32 + (block // 2) * ROWS, ROWS)
            parts.append(total[at, pl.ds((block % 2) * TILE, TILE)])
        peak = jnp.maximum(
            jnp.maximum(jnp.abs(parts[0]), jnp.abs(parts[1])),
            jnp.maximum(jnp.abs(parts[2]), jnp.abs(parts[3])),
        )
        scale = scale_of(jnp.max(peak, axis=1, keepdims=True))
        for block in range(4):
            codes = encode(parts[block], scale).astype(jnp.bfloat16)
            out_ref[dst, pl.ds(block * ROWS, ROWS), :] = codes
        sent = jnp.where(diagonal, scale * back_unit[...], 0.0)
        spread = jnp.sum(sent, axis=0, keepdims=True)
        plain = parts[0] * back_unit[...]
        long = jnp.where(diagonal, plain[:, 0:1], jnp.where(beside, plain[:, 1:2], 0.0))
        long = jnp.sum(long, axis=0, keepdims=True)
        ends = start_gate[dst : dst + 1, :] * long + start_base[dst : dst + 1, :]
        tail = jnp.where(tail_row == 0, spread, jnp.where(tail_row == 1, ends, 0.0))
        out_ref[dst, pl.ds(64, 8), :] = tail.astype(jnp.bfloat16)

    def lag_step(lag):
        rows = size - lag * ROWS
        part = jnp.dot(main[:rows, :], weight(toep, lag), preferred_element_type=jnp.float32)
        narrow = jnp.concatenate([weight(toep_narrow, lag), weight(toep_fine, lag)], axis=0)
        rest = jnp.dot(cross[:rows, :], narrow, preferred_element_type=jnp.float32)
        total[lag * ROWS :, :] += part + rest * (1.0 / FINE)

    def gate(piece, side):
        rows = slice(piece * 32, (piece + 1) * 32)
        local_rows = slice(piece % 4 * 32, piece % 4 * 32 + 32)
        gate_rows(streams, side, rows, local_rows, query_out, base_out)

    total[...] = jnp.zeros_like(total)
    toep[0] = jnp.zeros((TILE, TILE), toep.dtype)
    toep_narrow[0] = jnp.zeros((TILE, TILE), toep_narrow.dtype)
    toep_fine[0] = jnp.zeros((TILE, TILE), toep_fine.dtype)
    early = blocks * EARLY // 64
    ready = early // 2
    for src in range(ready):
        unpack(src)
    order = list(range(blocks - early, blocks)) + list(range(blocks - early))
    built = rolled(2 * order[0] - 1)
    built = build(2 * order[0] + 1, build(2 * order[0], build(2 * order[0] - 1, rolled(2 * order[0] - 2))))
    for index, lag in enumerate(order):
        if index + 1 < blocks:
            ahead = order[index + 1]
            if ahead == 0:
                built = jnp.zeros((TILE, TILE), jnp.float32)
            built = build(2 * ahead + 1, build(2 * ahead, built))
        lag_step(lag)
        while ready < min(count, early // 2 + (index + 1) * PER_STEP):
            unpack(ready)
            ready += 1
        place = index - early
        if place >= 0 and lag % 2 == 1:
            pack(lag // 2)
        if place >= GATE_FROM and (place - GATE_FROM) % GATE_STEP == 0:
            piece = (place - GATE_FROM) // GATE_STEP
            if piece < 16:
                if piece % 4 == 0:
                    cols = slice(piece * 32, piece * 32 + TILE)
                    side = side_columns([weight_ref[:, cols], skip_ref[:, cols]])
                gate(piece, side)
    for dst in range((blocks - early) // 2, count):
        pack(dst)


def conv(chunks, streams, weight, skip):
    count = chunks.shape[0]
    plane = jax.ShapeDtypeStruct(streams[0].shape, jnp.float32)
    size = count * 2 * ROWS
    tiles = (count * 4 + 1, TILE, TILE)
    whole = pl.BlockSpec(memory_space=pltpu.VMEM)
    return pl.pallas_call(
        conv_kernel,
        in_specs=[whole] * 6,
        out_specs=[whole] * 3,
        out_shape=[jax.ShapeDtypeStruct(chunks.shape, jnp.bfloat16), plane, plane],
        scratch_shapes=[
            pltpu.VMEM((size, 2 * TILE), jnp.bfloat16),
            pltpu.VMEM((size, 4 * TILE), jnp.float8_e4m3fn),
            pltpu.VMEM((count * 4, TILE), jnp.float32),
            pltpu.VMEM(tiles, jnp.bfloat16),
            pltpu.VMEM(tiles, jnp.float8_e4m3fn),
            pltpu.VMEM(tiles, jnp.float8_e4m3fn),
            pltpu.VMEM((size, 2 * TILE), jnp.float32),
            pltpu.VMEM((ROWS, TILE), jnp.float32),
            pltpu.VMEM((count, TILE), jnp.float32),
            pltpu.VMEM((count + 8, TILE), jnp.float32),
            pltpu.VMEM((count, TILE), jnp.float32),
            pltpu.VMEM((count, TILE), jnp.float32),
            pltpu.VMEM((count, TILE), jnp.float32),
        ],
        compiler_params=pltpu.CompilerParams(vmem_limit_bytes=24 * MIB),
        name="conv",
    )(chunks, *streams, weight, skip)


def back_kernel(in_ref, query_ref, base_ref, out_hbm, plain, starts, done, sent):
    lane = lax.broadcasted_iota(jnp.int32, (ROWS, TILE), 1)
    row = lax.broadcasted_iota(jnp.int32, (ROWS, TILE), 0)
    head = lax.broadcasted_iota(jnp.int32, (TILE, TILE), 1)
    copies = []
    for step in range(done.shape[0] // TILE):
        for filt in range(FILT):
            src = step * FILT + filt
            tail = in_ref[src, pl.ds(64, 8), :].astype(jnp.float32)
            scale = jnp.sum(jnp.where(lane == row, tail[0:1, :], 0.0), axis=1, keepdims=True)
            zero = jnp.sum(jnp.where(lane == row, tail[1:2, :], 0.0), axis=1, keepdims=True)
            one = jnp.where(lane == row + ROWS, tail[1:2, :], 0.0)
            one = jnp.sum(one, axis=1, keepdims=True)
            starts[step, pl.ds(filt, ROWS, stride=FILT), :] = jnp.where(lane == 0, zero, one)
            for block in range(4):
                part = in_ref[src, pl.ds(block * ROWS, ROWS), :].astype(jnp.float32)
                plain[step, block, pl.ds(filt, ROWS, stride=FILT), :] = decode(part, scale)
        rows = pl.ds(step * TILE, TILE)
        for block in range(4):
            cols = pl.ds(block * TILE, TILE)
            mixed = query_ref[rows, cols] * plain[step, block] + base_ref[rows, cols]
            if block == 0:
                mixed = jnp.where(head < 2, starts[step], mixed)
            done[rows, cols] = mixed.astype(jnp.bfloat16)
        copy = pltpu.make_async_copy(done.at[rows, :], out_hbm.at[rows, :], sent.at[step])
        copy.start()
        copies.append(copy)
    for copy in copies:
        copy.wait()


WHOLE = pl.BlockSpec(memory_space=pltpu.VMEM)


def whole_call(kernel, name, outs, *operands):
    return pl.pallas_call(
        kernel,
        in_specs=[WHOLE] * len(operands),
        out_specs=[WHOLE] * len(outs),
        out_shape=[jax.ShapeDtypeStruct(shape, dtype) for shape, dtype in outs],
        compiler_params=pltpu.CompilerParams(vmem_limit_bytes=16 * MIB),
        name=name,
    )(*operands)


def back(chunks, query_short, base):
    rows, length = base.shape
    steps = rows // TILE
    return pl.pallas_call(
        back_kernel,
        in_specs=[WHOLE] * 3,
        out_specs=pl.BlockSpec(memory_space=pl.ANY),
        out_shape=jax.ShapeDtypeStruct((rows, length), jnp.bfloat16),
        scratch_shapes=[
            pltpu.VMEM((steps, 4, TILE, TILE), jnp.float32),
            pltpu.VMEM((steps, TILE, TILE), jnp.float32),
            pltpu.VMEM((rows, length), jnp.bfloat16),
            pltpu.SemaphoreType.DMA((steps,)),
        ],
        compiler_params=pltpu.CompilerParams(vmem_limit_bytes=16 * MIB),
        name="back",
    )(chunks, query_short, base)


def local(query_proj, key_proj, value_proj, short_weight, skip_bias, filter_taps):
    count = lax.axis_size("context")
    rows, length = query_proj.shape
    taps = jnp.broadcast_to(filter_taps[:, None, :], (FILT, 1, length))
    taps = lax.all_to_all(taps, "tensor", 0, 0, tiled=True)
    weight = short_weight.reshape(9, rows)
    skip = skip_bias[None, :]
    outs = [
        ((4, rows, TILE), jnp.float32),
        ((count, TILE), jnp.float32),
        ((2, count, TILE), jnp.float32),
    ]
    streams = (key_proj, value_proj)
    coded, scales, ends = whole_call(front_kernel, "front", outs, *streams, weight)
    outs = [((count, CHUNK, TILE), jnp.bfloat16)]
    (chunks,) = whole_call(deal_kernel, "deal", outs, coded, scales, ends, query_proj, taps)
    chunks = lax.all_to_all(chunks, "context", 0, 0, tiled=True)
    streams = (query_proj, key_proj, value_proj)
    chunks, query_short, base = conv(chunks, streams, weight, skip)
    chunks = lax.all_to_all(chunks, "context", 0, 0, tiled=True)
    return back(chunks, query_short, base)


def solution(mesh):
    in_specs = (
        P("tensor", "context"),
        P("tensor", "context"),
        P("tensor", "context"),
        P(None, None, "tensor"),
        P("tensor"),
        P("tensor", "context"),
    )
    out_specs = P("tensor", "context")
    return jax.shard_map(local, mesh=mesh, in_specs=in_specs, out_specs=out_specs, check_vma=False)
```

```python
import jax
import jax.numpy as jnp
from jax import lax
from jax.experimental import pallas as pl
from jax.experimental.pallas import tpu as pltpu
from jax.sharding import PartitionSpec as P

FILT = 8
TILE = 128
ROWS = 16
CHUNK = 72
GAIN = 16.0
SLOPE = 61.0
LIFT = 125.0
TINY = 1e-30
MIB = 1024 * 1024


def scale_of(peak):
    return jnp.maximum(peak, TINY).astype(jnp.bfloat16).astype(jnp.float32)


def encode(values, scale):
    level = jnp.log2(1.0 + jnp.abs(values) * (GAIN / scale))
    size = jnp.exp2(level * SLOPE - LIFT)
    return jnp.where(values < 0.0, -size, size)


def decode(codes, scale):
    level = (jnp.log2(jnp.abs(codes)) + LIFT) * (1.0 / SLOPE)
    size = (jnp.exp2(level) - 1.0) * (scale * (1.0 / GAIN))
    return jnp.where(codes < 0.0, -size, size)


def split(values):
    high = values.astype(jnp.bfloat16)
    low = (values - high.astype(jnp.float32)).astype(jnp.bfloat16)
    return high, low


def short_mix(stream, weights):
    one = pltpu.roll(stream, 1, 1)
    two = pltpu.roll(stream, 2, 1)
    return weights[0] * stream + weights[1] * one + weights[2] * two


def to_lanes(column):
    shape = (TILE, TILE)
    lane = lax.broadcasted_iota(jnp.int32, shape, 1)
    group = lax.broadcasted_iota(jnp.int32, shape, 0) // FILT
    spread = jnp.where(lane == group, column, 0.0)
    return spread.reshape(ROWS, FILT, TILE).sum(axis=0)


def side_columns(rows):
    missing = 16 - sum(part.shape[0] for part in rows)
    rows = rows + [jnp.zeros((missing, TILE), jnp.float32)]
    return jnp.transpose(jnp.concatenate(rows, axis=0))


def product_of(key_ref, value_ref, side, rows):
    key = key_ref[rows, :].astype(jnp.float32)
    value = value_ref[rows, :].astype(jnp.float32)
    key_short = short_mix(key, [side[:, n : n + 1] for n in range(3, 6)])
    value_short = short_mix(value, [side[:, n : n + 1] for n in range(6, 9)])
    return key_short * value_short


def ends_of(refs, start):
    shape = (TILE, TILE)
    lane = lax.broadcasted_iota(jnp.int32, shape, 1)
    place = lax.broadcasted_iota(jnp.int32, shape, 0)
    total = None
    for index, ref in enumerate(refs):
        pick = (lane // 32 == index) & (place == start % TILE + lane % 32 // 16)
        part = jnp.dot(
            ref[:, start // TILE * TILE : start // TILE * TILE + TILE],
            pick.astype(jnp.bfloat16),
            preferred_element_type=jnp.float32,
        )
        total = part if total is None else total + part
    return total


def ends_rows(both, step):
    group = lax.broadcasted_iota(jnp.int32, (TILE, TILE), 0) // FILT
    own = lax.broadcasted_iota(jnp.int32, (TILE, TILE), 1) % ROWS == group
    rows = slice(step * TILE, (step + 1) * TILE)
    spread = [jnp.where(own, part[rows, :], 0.0) for part in both]
    return [part.reshape(ROWS, FILT, TILE).sum(axis=0) for part in spread]


def front_kernel(key_ref, value_ref, weight_ref, coded_ref, scale_ref):
    length = key_ref.shape[1]
    lane = lax.broadcasted_iota(jnp.int32, (TILE, length), 1)
    for step in range(key_ref.shape[0] // TILE):
        rows = slice(step * TILE, (step + 1) * TILE)
        dests = slice(step * FILT, (step + 1) * FILT)
        side = side_columns([weight_ref[:, rows]])
        product = jnp.where(lane < 2, 0.0, product_of(key_ref, value_ref, side, rows))
        scale = scale_of(jnp.max(jnp.abs(product), axis=1, keepdims=True))
        coded_rows = encode(product, scale)
        for block in range(4):
            coded_ref[block, rows, :] = coded_rows[:, block * TILE : (block + 1) * TILE]
        scale_ref[dests, :] = to_lanes(scale)


def deal_kernel(coded_ref, scale_ref, key_ref, value_ref, query_ref, taps_ref, out_ref):
    refs = (key_ref, value_ref, query_ref)
    both = [ends_of(refs, start) for start in (0, query_ref.shape[1] - 2)]
    row = lax.broadcasted_iota(jnp.int32, (8, TILE), 0)
    tails = []
    for filt in range(FILT):
        taps = taps_ref[filt]
        tap_scale = scale_of(jnp.max(jnp.abs(taps)))
        tail = jnp.where(row == 5, tap_scale, 0.0)
        codes = encode(taps, tap_scale)
        for block in range(4):
            part = codes[:, block * TILE : (block + 1) * TILE]
            tail = jnp.where(row == block, part, tail)
        tails.append(tail)
    for dest in range(out_ref.shape[0]):
        step, filt = dest // FILT, dest % FILT
        if filt == 0:
            late = ends_rows(both, step)
        for block in range(4):
            rows = pl.ds(step * TILE + filt, ROWS, stride=FILT)
            part = coded_ref[block, rows, :]
            out_ref[dest, block * ROWS : (block + 1) * ROWS, :] = part.astype(jnp.bfloat16)
        tail = jnp.where(row == 4, scale_ref[dest : dest + 1, :], tails[filt])
        ends = late[0][filt : filt + 1, :]
        tail = jnp.where(row == 6, ends, tail)
        ends = late[1][filt : filt + 1, :]
        tail = jnp.where(row == 7, ends, tail)
        out_ref[dest, 64:72, :] = tail.astype(jnp.bfloat16)


def gate_rows(streams, side, rows, local, query_out, base_out):
    query_ref, key_ref, value_ref = streams
    side = side[local, :]
    query = query_ref[rows, :].astype(jnp.float32)
    query_short = short_mix(query, [side[:, n : n + 1] for n in range(3)])
    query_out[rows, :] = query_short
    product = product_of(key_ref, value_ref, side, rows)
    base_out[rows, :] = query_short * (side[:, 9:10] * product)


FINE = 512.0
GATE_FROM = 0
GATE_STEP = 1
EARLY = 4
PER_STEP = 8


def unit_of(peak):
    power = jnp.exp2(7.0 - jnp.ceil(jnp.log2(jnp.maximum(peak, TINY))))
    return power.astype(jnp.bfloat16).astype(jnp.float32)


def four_parts(values):
    coarse = values.astype(jnp.bfloat16)
    wide = coarse.astype(jnp.float32)
    narrow = wide.astype(jnp.float8_e4m3fn)
    fine = ((values - wide) * FINE).astype(jnp.float8_e4m3fn)
    return coarse, narrow, fine


def own_weights(weight_ref, skip_ref):
    index = lax.axis_index("context")
    cols = pl.ds(pl.multiple_of(index // FILT * TILE, TILE), TILE)
    source = lax.broadcasted_iota(jnp.int32, (TILE, TILE), 0)
    lane = lax.broadcasted_iota(jnp.int32, (TILE, TILE), 1)
    pick = (source % FILT == index % FILT) & (source // FILT == lane % ROWS)
    zeros = jnp.zeros((6, TILE), jnp.float32)
    rows = jnp.concatenate([weight_ref[:, cols], skip_ref[:, cols], zeros], axis=0)
    return jnp.dot(
        rows,
        pick.astype(jnp.float32),
        precision=lax.Precision.HIGHEST,
        preferred_element_type=jnp.float32,
    )


def start_mix(first, before, weights):
    lane = lax.broadcasted_iota(jnp.int32, first.shape, 1)
    taps = []
    for lag in range(3):
        query, key, value = [weights[3 * n + lag : 3 * n + lag + 1, :] for n in range(3)]
        taps.append(jnp.where(lane < 32, key, jnp.where(lane < 64, value, query)))
    second = lane % 32 >= ROWS
    one = jnp.where(second, pltpu.roll(first, ROWS, 1), pltpu.roll(before, TILE - ROWS, 1))
    return taps[0] * first + taps[1] * one + taps[2] * before, weights[9:10, :]


def conv_kernel(
    in_ref,
    query_ref,
    key_ref,
    value_ref,
    weight_ref,
    skip_ref,
    out_ref,
    query_out,
    base_out,
    main,
    cross,
    taps,
    toep,
    toep_narrow,
    toep_fine,
    total,
    back_unit,
    first,
    last,
    start_prod,
    start_gate,
    start_base,
):
    streams = (query_ref, key_ref, value_ref)
    count = in_ref.shape[0]
    blocks = count * 2
    size = blocks * ROWS
    lane = lax.broadcasted_iota(jnp.int32, (ROWS, TILE), 1)
    row = lax.broadcasted_iota(jnp.int32, (ROWS, TILE), 0)
    diagonal = lane == row
    beside = lane == row + ROWS
    tail_row = lax.broadcasted_iota(jnp.int32, (8, TILE), 0)
    wide_lane = lax.broadcasted_iota(jnp.int32, (TILE, TILE), 1)
    causal = wide_lane >= lax.broadcasted_iota(jnp.int32, (TILE, TILE), 0)

    def tail_of(src):
        return in_ref[src, pl.ds(64, 8), :].astype(jnp.float32)

    last[0:1, :] = jnp.zeros((1, TILE), jnp.float32)
    peaks = None
    for src in range(count):
        tail = tail_of(src)
        peaks = tail if peaks is None else jnp.maximum(peaks, tail)
        taps[src * 4 : (src + 1) * 4, :] = decode(tail[0:4, :], tail[5:6, :])
        first[src : src + 1, :] = tail[6:7, :]
        last[src + 1 : src + 2, :] = tail[7:8, :]
    lane_weights = own_weights(weight_ref, skip_ref)
    mixed, skip = start_mix(first[...], last[0:count, :], lane_weights)
    product = mixed * pltpu.roll(mixed, TILE - 32, 1)
    query = pltpu.roll(mixed, TILE - 64, 1)
    start_prod[...] = product
    start_gate[...] = query
    start_base[...] = query * (skip * product)

    def column(mask, line):
        return jnp.sum(jnp.where(mask, line, 0.0), axis=1, keepdims=True)

    start_peak = jnp.max(jnp.abs(product), axis=0, keepdims=True)
    start_peak = jnp.maximum(column(diagonal, start_peak), column(beside, start_peak))
    unit = unit_of(jnp.maximum(column(diagonal, peaks[4:5, :]), start_peak))
    tap_unit = unit_of(peaks[5:6, 0:1])
    back_unit[...] = jnp.broadcast_to(1.0 / (unit * tap_unit), (ROWS, TILE))

    def unpack(src):
        tail = tail_of(src)
        scale = column(diagonal, tail[4:5, :]) * unit
        starts = start_prod[src : src + 1, :]
        early = jnp.where(lane == 0, column(diagonal, starts), column(beside, starts)) * unit
        at = slice(src * 32, (src + 1) * 32)
        for half in range(2):
            pair = []
            for block in (half, half + 2):
                part = in_ref[src, pl.ds(block * ROWS, ROWS), :].astype(jnp.float32)
                values = decode(part, scale)
                pair.append(jnp.where(lane < 2, early, values) if block == 0 else values)
            coarse, narrow, fine = four_parts(jnp.concatenate(pair, axis=0))
            main[at, pl.ds(half * TILE, TILE)] = coarse
            cross[at, pl.ds(half * TILE, TILE)] = fine
            cross[at, pl.ds((half + 2) * TILE, TILE)] = narrow

    def rolled(tile):
        line = jnp.broadcast_to(taps[tile : tile + 1, :] * tap_unit, (TILE, TILE))
        return pltpu.roll(line, 0, 1, stride=1, stride_axis=0)

    def build(tile, before):
        here = rolled(tile)
        coarse, narrow, fine = four_parts(jnp.where(causal, here, before))
        toep[tile + 1] = coarse
        toep_narrow[tile + 1] = narrow
        toep_fine[tile + 1] = fine
        return here

    def weight(ref, lag):
        top = jnp.concatenate([ref[2 * lag + 1], ref[2 * lag + 2]], axis=1)
        bottom = jnp.concatenate([ref[2 * lag], ref[2 * lag + 1]], axis=1)
        return jnp.concatenate([top, bottom], axis=0)

    def pack(dst):
        parts = []
        for block in range(4):
            at = pl.ds(dst * 32 + (block // 2) * ROWS, ROWS)
            parts.append(total[at, pl.ds((block % 2) * TILE, TILE)])
        peak = jnp.maximum(
            jnp.maximum(jnp.abs(parts[0]), jnp.abs(parts[1])),
            jnp.maximum(jnp.abs(parts[2]), jnp.abs(parts[3])),
        )
        scale = scale_of(jnp.max(peak, axis=1, keepdims=True))
        for block in range(4):
            codes = encode(parts[block], scale).astype(jnp.bfloat16)
            out_ref[dst, pl.ds(block * ROWS, ROWS), :] = codes
        sent = jnp.where(diagonal, scale * back_unit[...], 0.0)
        spread = jnp.sum(sent, axis=0, keepdims=True)
        plain = parts[0] * back_unit[...]
        long = jnp.where(diagonal, plain[:, 0:1], jnp.where(beside, plain[:, 1:2], 0.0))
        long = jnp.sum(long, axis=0, keepdims=True)
        ends = start_gate[dst : dst + 1, :] * long + start_base[dst : dst + 1, :]
        tail = jnp.where(tail_row == 0, spread, jnp.where(tail_row == 1, ends, 0.0))
        out_ref[dst, pl.ds(64, 8), :] = tail.astype(jnp.bfloat16)

    def lag_step(lag):
        rows = size - lag * ROWS
        part = jnp.dot(main[:rows, :], weight(toep, lag), preferred_element_type=jnp.float32)
        narrow = jnp.concatenate([weight(toep_narrow, lag), weight(toep_fine, lag)], axis=0)
        rest = jnp.dot(cross[:rows, :], narrow, preferred_element_type=jnp.float32)
        total[lag * ROWS :, :] += part + rest * (1.0 / FINE)

    def gate(piece, side):
        rows = slice(piece * 32, (piece + 1) * 32)
        local_rows = slice(piece % 4 * 32, piece % 4 * 32 + 32)
        gate_rows(streams, side, rows, local_rows, query_out, base_out)

    total[...] = jnp.zeros_like(total)
    toep[0] = jnp.zeros((TILE, TILE), toep.dtype)
    toep_narrow[0] = jnp.zeros((TILE, TILE), toep_narrow.dtype)
    toep_fine[0] = jnp.zeros((TILE, TILE), toep_fine.dtype)
    early = blocks * EARLY // 64
    ready = early // 2
    for src in range(ready):
        unpack(src)
    order = list(range(blocks - early, blocks)) + list(range(blocks - early))
    built = rolled(2 * order[0] - 1)
    built = build(2 * order[0] + 1, build(2 * order[0], build(2 * order[0] - 1, rolled(2 * order[0] - 2))))
    for index, lag in enumerate(order):
        if index + 1 < blocks:
            ahead = order[index + 1]
            if ahead == 0:
                built = jnp.zeros((TILE, TILE), jnp.float32)
            built = build(2 * ahead + 1, build(2 * ahead, built))
        lag_step(lag)
        while ready < min(count, early // 2 + (index + 1) * PER_STEP):
            unpack(ready)
            ready += 1
        place = index - early
        if place >= 0 and lag % 2 == 1:
            pack(lag // 2)
        if place >= GATE_FROM and (place - GATE_FROM) % GATE_STEP == 0:
            piece = (place - GATE_FROM) // GATE_STEP
            if piece < 16:
                if piece % 4 == 0:
                    cols = slice(piece * 32, piece * 32 + TILE)
                    side = side_columns([weight_ref[:, cols], skip_ref[:, cols]])
                gate(piece, side)
    for dst in range((blocks - early) // 2, count):
        pack(dst)


def conv(chunks, streams, weight, skip):
    count = chunks.shape[0]
    plane = jax.ShapeDtypeStruct(streams[0].shape, jnp.float32)
    size = count * 2 * ROWS
    tiles = (count * 4 + 1, TILE, TILE)
    whole = pl.BlockSpec(memory_space=pltpu.VMEM)
    return pl.pallas_call(
        conv_kernel,
        in_specs=[whole] * 6,
        out_specs=[whole] * 3,
        out_shape=[jax.ShapeDtypeStruct(chunks.shape, jnp.bfloat16), plane, plane],
        scratch_shapes=[
            pltpu.VMEM((size, 2 * TILE), jnp.bfloat16),
            pltpu.VMEM((size, 4 * TILE), jnp.float8_e4m3fn),
            pltpu.VMEM((count * 4, TILE), jnp.float32),
            pltpu.VMEM(tiles, jnp.bfloat16),
            pltpu.VMEM(tiles, jnp.float8_e4m3fn),
            pltpu.VMEM(tiles, jnp.float8_e4m3fn),
            pltpu.VMEM((size, 2 * TILE), jnp.float32),
            pltpu.VMEM((ROWS, TILE), jnp.float32),
            pltpu.VMEM((count, TILE), jnp.float32),
            pltpu.VMEM((count + 8, TILE), jnp.float32),
            pltpu.VMEM((count, TILE), jnp.float32),
            pltpu.VMEM((count, TILE), jnp.float32),
            pltpu.VMEM((count, TILE), jnp.float32),
        ],
        compiler_params=pltpu.CompilerParams(vmem_limit_bytes=24 * MIB),
        name="conv",
    )(chunks, *streams, weight, skip)


def back_kernel(in_ref, query_ref, base_ref, out_hbm, plain, starts, done, sent):
    lane = lax.broadcasted_iota(jnp.int32, (ROWS, TILE), 1)
    row = lax.broadcasted_iota(jnp.int32, (ROWS, TILE), 0)
    head = lax.broadcasted_iota(jnp.int32, (TILE, TILE), 1)
    copies = []
    for step in range(done.shape[0] // TILE):
        for filt in range(FILT):
            src = step * FILT + filt
            tail = in_ref[src, pl.ds(64, 8), :].astype(jnp.float32)
            scale = jnp.sum(jnp.where(lane == row, tail[0:1, :], 0.0), axis=1, keepdims=True)
            zero = jnp.sum(jnp.where(lane == row, tail[1:2, :], 0.0), axis=1, keepdims=True)
            one = jnp.where(lane == row + ROWS, tail[1:2, :], 0.0)
            one = jnp.sum(one, axis=1, keepdims=True)
            starts[step, pl.ds(filt, ROWS, stride=FILT), :] = jnp.where(lane == 0, zero, one)
            for block in range(4):
                part = in_ref[src, pl.ds(block * ROWS, ROWS), :].astype(jnp.float32)
                plain[step, block, pl.ds(filt, ROWS, stride=FILT), :] = decode(part, scale)
        rows = pl.ds(step * TILE, TILE)
        for block in range(4):
            cols = pl.ds(block * TILE, TILE)
            mixed = query_ref[rows, cols] * plain[step, block] + base_ref[rows, cols]
            if block == 0:
                mixed = jnp.where(head < 2, starts[step], mixed)
            done[rows, cols] = mixed.astype(jnp.bfloat16)
        copy = pltpu.make_async_copy(done.at[rows, :], out_hbm.at[rows, :], sent.at[step])
        copy.start()
        copies.append(copy)
    for copy in copies:
        copy.wait()


WHOLE = pl.BlockSpec(memory_space=pltpu.VMEM)


def whole_call(kernel, name, outs, *operands):
    return pl.pallas_call(
        kernel,
        in_specs=[WHOLE] * len(operands),
        out_specs=[WHOLE] * len(outs),
        out_shape=[jax.ShapeDtypeStruct(shape, dtype) for shape, dtype in outs],
        compiler_params=pltpu.CompilerParams(vmem_limit_bytes=16 * MIB),
        name=name,
    )(*operands)


def back(chunks, query_short, base):
    rows, length = base.shape
    steps = rows // TILE
    return pl.pallas_call(
        back_kernel,
        in_specs=[WHOLE] * 3,
        out_specs=pl.BlockSpec(memory_space=pl.ANY),
        out_shape=jax.ShapeDtypeStruct((rows, length), jnp.bfloat16),
        scratch_shapes=[
            pltpu.VMEM((steps, 4, TILE, TILE), jnp.float32),
            pltpu.VMEM((steps, TILE, TILE), jnp.float32),
            pltpu.VMEM((rows, length), jnp.bfloat16),
            pltpu.SemaphoreType.DMA((steps,)),
        ],
        compiler_params=pltpu.CompilerParams(vmem_limit_bytes=16 * MIB),
        name="back",
    )(chunks, query_short, base)


def local(query_proj, key_proj, value_proj, short_weight, skip_bias, filter_taps):
    count = lax.axis_size("context")
    rows, length = query_proj.shape
    taps = jnp.broadcast_to(filter_taps[:, None, :], (FILT, 1, length))
    taps = lax.all_to_all(taps, "tensor", 0, 0, tiled=True)
    weight = short_weight.reshape(9, rows)
    skip = skip_bias[None, :]
    outs = [
        ((4, rows, TILE), jnp.float32),
        ((count, TILE), jnp.float32),
    ]
    streams = (key_proj, value_proj)
    coded, scales = whole_call(front_kernel, "front", outs, *streams, weight)
    outs = [((count, CHUNK, TILE), jnp.bfloat16)]
    (chunks,) = whole_call(deal_kernel, "deal", outs, coded, scales, *streams, query_proj, taps)
    chunks = lax.all_to_all(chunks, "context", 0, 0, tiled=True)
    streams = (query_proj, key_proj, value_proj)
    chunks, query_short, base = conv(chunks, streams, weight, skip)
    chunks = lax.all_to_all(chunks, "context", 0, 0, tiled=True)
    return back(chunks, query_short, base)


def solution(mesh):
    in_specs = (
        P("tensor", "context"),
        P("tensor", "context"),
        P("tensor", "context"),
        P(None, None, "tensor"),
        P("tensor"),
        P("tensor", "context"),
    )
    out_specs = P("tensor", "context")
    return jax.shard_map(local, mesh=mesh, in_specs=in_specs, out_specs=out_specs, check_vma=False)
```
